128 devices in a mesh: sess: 16 (over y, x), mp: 8 (over z, core).
Axes of the slice: x: 4, y: 4, z: 4, core: 2. Of those that a mesh axis runs over, the one named last changes fastest.
Arguments:
- mamba_x: bfloat16 [8192, 8192], P('sess', 'mp')
- gate_z: bfloat16 [8192, 8192], P('sess', 'mp'), may hold values from -6 to 6
- proj_bc: bfloat16 [8192, 2, 4, 256], P('sess'), may hold values from -6 to 6
- step_raw: float32 [128, 8192], P('mp', 'sess')
- step_bias: float32 [128], P('mp'), may hold values from -4.5 to -3.5
- decay_log: float32 [128], P('mp')
- skip_gain: float32 [128], P('mp'), may hold values from 0.5 to 1.5
- norm_gain: float32 [8192], P('mp'), may hold values from 0.1 to 1.9
- state_cache: bfloat16 [256, 128, 64, 256], P('sess', 'mp'), may hold values from -1.1953125 to 1.1953125
- cache_slot: int32 [256], replicated, may hold values from 0 to 255, as said below
- prefix_pages: int32 [256], P('sess'), may hold values from 1 to 4
- page_table: int32 [256, 4], replicated, may hold values from 0 to 63, as said below
- queries: bfloat16 [8192, 8192], P('sess', 'mp')
- appended_memory_pair: bfloat16 [8192, 2, 8, 128], P('sess', None, 'mp')
- key_value_pages: bfloat16 [1024, 64, 2, 8, 128], P('sess', None, None, 'mp'), may hold values from -6 to 6
Outputs:
- mamba_out: bfloat16 [8192, 8192], P('sess', 'mp')
- new_state: bfloat16 [256, 128, 64, 256], P('sess', 'mp')
- attn_out: bfloat16 [8192, 8192], P('sess', 'mp')
The draws below stay inside these ranges and needn't reach their ends.
Inputs may be any that keep to these rules, and one draw needn't show every extreme that they name: cache_slot is a permutation of the 256 slots; slot c is held by the owner c // 16 on sess at local slot c % 16; among the 16 sessions of one index of sess at most 2 have their caches on one owner, and that many do in every draw. `page_table`: entries are page indices in the pool of the session's owner; the 4 entries of a session are distinct and no page serves two sessions.
All inputs are finite; a program needn't handle non-finite values.
Results may differ from the reference program's by a relative error of at most 0.0049.
Values may be sent and summed in bfloat16 or wider, within the bound.
No kernel may reach another device: no remote copies, remote signals or barrier semaphores. Data moves between devices by JAX's collectives and lax.ppermute only.
A program may use at most 192 MiB of HBM per device.

```python
import jax
import jax.numpy as jnp
from jax import lax

HM = 128
P_SIZE = 64
NS = 256
G = 4
QUERY_HEADS = 64
KEY_VALUE_HEADS = 8
HEAD_WIDTH = 128
S_DEV = 16
SESSION_TOKENS = 32
PAGE_TOKENS = 64
LONGEST_PAGES = 4
SESSION_COUNT = 256
ADDED_ITEM_TALLY = 8192
POOLP = 64
TOTAL_PAGES = 1024


def route_slots(key):
    blocks = SESSION_COUNT // S_DEV
    shift_key, owner_key, pick_key, order_key = jax.random.split(jax.random.fold_in(key, 101), 4)
    shifts = jax.random.permutation(shift_key, blocks)
    relabel = jax.random.permutation(owner_key, blocks)
    others = jnp.concatenate([shifts[1:], shifts[1:]])
    mixed = jax.random.permutation(pick_key, others.shape[0])
    chosen = others[mixed][:S_DEV - 2]
    offsets = jnp.concatenate([shifts[:1], shifts[:1], chosen])
    device = jnp.arange(blocks)[:, None]
    owners = relabel[(device + offsets[None, :]) % blocks]

    def shuffle(subkey):
        return jax.random.permutation(subkey, S_DEV)
    orders = jax.vmap(shuffle)(jax.random.split(order_key, blocks))
    placed = jnp.take_along_axis(owners, orders, axis=1)
    return (placed * S_DEV + orders).reshape(-1).astype(jnp.int32)


def draw_cache_slot(key, part):
    return route_slots(key)


def draw_page_table(key, part):
    slots = route_slots(key)
    key = jax.random.fold_in(key, 7)
    blocks = SESSION_COUNT // S_DEV

    def shuffle(subkey):
        return jax.random.permutation(subkey, POOLP)
    pools = jax.vmap(shuffle)(jax.random.split(key, blocks))
    owner = slots // S_DEV
    local = slots % S_DEV
    columns = local[:, None] * LONGEST_PAGES + jnp.arange(LONGEST_PAGES)[None, :]
    return pools[owner[:, None], columns].astype(jnp.int32)


def draw_prefix_pages(key, part):
    key = jax.random.fold_in(key, 13)
    count_key, pick_key = jax.random.split(key)
    counts = jax.random.randint(count_key, (SESSION_COUNT,), 1, LONGEST_PAGES + 1)
    longest = jax.random.randint(pick_key, (), 0, SESSION_COUNT)
    return jnp.where(jnp.arange(SESSION_COUNT) == longest, LONGEST_PAGES, counts).astype(jnp.int32)


def draw_step_raw(key, part):
    key = jax.random.fold_in(key, 21)
    seed_generator_root, spike_generator_seed = jax.random.split(key)
    starting_shift = jnp.clip(0.7 * jax.random.normal(seed_generator_root, (HM, ADDED_ITEM_TALLY), jnp.float32), -4.2, 4.2)
    arrival_spike = jax.random.randint(spike_generator_seed, (1, ADDED_ITEM_TALLY), 0, 40) == 0
    return starting_shift + jnp.where(arrival_spike, 5.0, 0.0)


def draw_decay_log(key, part):
    key = jax.random.fold_in(key, 23)
    return jax.random.uniform(key, (HM,), jnp.float32, -2.3, 0.4)


def draw_mamba_x(key, part):
    key = jax.random.fold_in(key, 31)
    seed_generator_root, row_key, col_key = jax.random.split(key, 3)
    row_scale = jnp.exp(jax.random.uniform(row_key, (ADDED_ITEM_TALLY, 1), jnp.float32, 0.0, 2.3))
    head_number = jnp.arange(HM * P_SIZE) // P_SIZE
    place = (head_number % (HM // G)).astype(jnp.float32) / (HM // G)
    col_scale = 3.0 ** place * jnp.exp(jax.random.uniform(col_key, (HM,), jnp.float32, -0.7, 0.7))[head_number]
    starting_shift = jnp.clip(jax.random.normal(seed_generator_root, (ADDED_ITEM_TALLY, HM * P_SIZE), jnp.float32), -4.0, 4.0)
    return (starting_shift * row_scale * col_scale[None, :] / 6.0).astype(jnp.bfloat16)


def draw_queries(key, part):
    key = jax.random.fold_in(key, 41)
    return jnp.clip(jax.random.normal(key, (ADDED_ITEM_TALLY, QUERY_HEADS * HEAD_WIDTH), jnp.float32), -6.0, 6.0).astype(jnp.bfloat16)


def draw_appended_memory_pair(key, part):
    key = jax.random.fold_in(key, 43)
    return jnp.clip(jax.random.normal(key, (ADDED_ITEM_TALLY, 2, KEY_VALUE_HEADS, HEAD_WIDTH), jnp.float32), -6.0, 6.0).astype(jnp.bfloat16)


def block_levels(own_key, extent, pieces, least, top_value):
    loudness, own = 1.0, jax.random.fold_in(own_key, 6)
    for axis_at, shards_of in pieces:
        steps = jnp.exp(jax.random.uniform(jax.random.fold_in(own, axis_at), (shards_of,), jnp.float32, least / len(pieces), top_value / len(pieces)))
        loudness = loudness * jnp.repeat(steps, extent[axis_at] // shards_of).reshape([-1 if axis == axis_at else 1 for axis in range(len(extent))])
    return loudness


def bell_draw(rng, extent, width, most, shards=(), kind=jnp.bfloat16):
    level = block_levels(rng, extent, shards, -0.22, 0.18) if shards else 1.0
    drawn = jax.random.normal(rng, extent, jnp.float32) * width * level
    return jnp.minimum(jnp.maximum(drawn, -most), most).astype(kind)


def setup_inputs(seed: int = 0) -> dict:
    key_of = jax.random.split(jax.random.key(seed), 16)
    return {
        "mamba_x": draw_mamba_x(jax.random.fold_in(key_of[15], 71), 0),
        "gate_z": bell_draw(key_of[1], (ADDED_ITEM_TALLY, HM * P_SIZE), 1.0, 6.0, ((0, 16), (1, 8))),
        "proj_bc": bell_draw(key_of[2], (ADDED_ITEM_TALLY, 2, G, NS), 1.0, 6.0, ((0, 16),)),
        "step_raw": draw_step_raw(jax.random.fold_in(key_of[15], 71), 0),
        "step_bias": jnp.clip(-4.5 + 1.0 * jax.random.uniform(key_of[4], (HM,), jnp.float32) ** block_levels(key_of[4], (HM,), ((0, 8),), -0.2, 0.2), -4.5, -3.5),
        "decay_log": draw_decay_log(jax.random.fold_in(key_of[15], 71), 0),
        "skip_gain": jnp.clip(0.5 + 1.0 * jax.random.uniform(key_of[6], (HM,), jnp.float32) ** block_levels(key_of[6], (HM,), ((0, 8),), -0.2, 0.2), 0.5, 1.5),
        "norm_gain": jnp.clip(1.0 + 0.18 * jax.random.normal(key_of[7], (HM * P_SIZE,), jnp.float32), 0.1, 1.9),
        "state_cache": bell_draw(key_of[8], (SESSION_COUNT, HM, P_SIZE, NS), 0.2, 1.1953125, ((0, 16), (1, 8))),
        "cache_slot": draw_cache_slot(jax.random.fold_in(key_of[15], 71), 0),
        "prefix_pages": draw_prefix_pages(jax.random.fold_in(key_of[15], 71), 0),
        "page_table": draw_page_table(jax.random.fold_in(key_of[15], 71), 0),
        "queries": draw_queries(jax.random.fold_in(key_of[15], 71), 0),
        "appended_memory_pair": draw_appended_memory_pair(jax.random.fold_in(key_of[15], 71), 0),
        "key_value_pages": bell_draw(key_of[14], (TOTAL_PAGES, PAGE_TOKENS, 2, KEY_VALUE_HEADS, HEAD_WIDTH), 1.0, 6.0, ((0, 16), (3, 8))),
    }


EPS = 1e-05

def mamba_session(values, gates, proj, raw_steps, start, step_bias, decay_log, skip_gain, norm_gain):
    prefix_length = values.shape[0]
    per_group = HM // G
    member = jnp.arange(HM) // per_group
    delta = jax.nn.softplus(raw_steps + step_bias[:, None])
    falloff_factor = -jnp.exp(decay_log)[:, None] * delta
    position = jnp.arange(prefix_length)
    lower = (position[:, None] >= position[None, :]).astype(jnp.float32)
    cumul = jnp.dot(falloff_factor, lower.T, precision=lax.Precision.HIGHEST)
    causal = lower > 0
    spread = cumul[:, :, None] - cumul[:, None, :]
    decay = jnp.where(causal[None], jnp.exp(jnp.where(causal[None], spread, 0.0)), 0.0)
    inputs_b = proj[:, 0].astype(jnp.float32)
    inputs_c = proj[:, 1].astype(jnp.float32)
    inner = jnp.einsum('tgn,ugn->gtu', inputs_c, inputs_b)[member]
    weights = (inner * decay * delta[:, None, :]).astype(jnp.bfloat16)
    heads_x = values.reshape(prefix_length, HM, P_SIZE).astype(jnp.float32)
    intra = jnp.einsum('htu,uhp->thp', weights.astype(jnp.float32), heads_x)
    c_heads = inputs_c[:, member]
    carried = jnp.einsum('thn,hpn->thp', c_heads, start.astype(jnp.float32))
    output = intra + carried * jnp.exp(cumul).T[:, :, None] + skip_gain[None, :, None] * heads_x
    gated = output * jax.nn.silu(gates.reshape(prefix_length, HM, P_SIZE).astype(jnp.float32))
    grouped = gated.reshape(prefix_length, G, per_group * P_SIZE)
    meansq = lax.optimization_barrier(jnp.mean(grouped * grouped, axis=2, keepdims=True))
    normed = (grouped * lax.rsqrt(meansq + EPS)).reshape(prefix_length, HM * P_SIZE) * norm_gain[None, :]
    tail = jnp.exp(cumul[:, -1:] - cumul) * delta
    scaled = (heads_x * tail.T[:, :, None]).astype(jnp.bfloat16)
    b_heads = inputs_b[:, member]
    local = jnp.einsum('thp,thn->hpn', scaled.astype(jnp.float32), b_heads)
    fresh = jnp.exp(cumul[:, -1])[:, None, None] * start.astype(jnp.float32) + local
    return (normed.astype(jnp.bfloat16), fresh.astype(jnp.bfloat16))

def attend_session(requested, fresh_kv, page_key_value, npages):
    prefix_length = requested.shape[0]
    keyvals = jnp.concatenate([page_key_value, fresh_kv], axis=0).astype(jnp.float32)
    kept = page_key_value.shape[0]
    query_rows = requested.reshape(prefix_length, KEY_VALUE_HEADS, QUERY_HEADS // KEY_VALUE_HEADS, HEAD_WIDTH).astype(jnp.float32)
    scores = jnp.einsum('tkgd,jkd->kgtj', query_rows, keyvals[:, 0]) * HEAD_WIDTH ** (-0.5)
    column = jnp.arange(kept + prefix_length)
    row = jnp.arange(prefix_length)
    valid = jnp.where(column[None, :] < kept, column[None, :] < npages * PAGE_TOKENS, column[None, :] - kept <= row[:, None])
    scores = jnp.where(valid[None, None], scores, -jnp.inf)
    peak = lax.optimization_barrier(jnp.max(scores, axis=-1, keepdims=True))
    expo = jnp.exp(scores - peak)
    probs = (expo / lax.optimization_barrier(jnp.sum(expo, axis=-1, keepdims=True))).astype(jnp.bfloat16)
    mixed = jnp.einsum('kgtj,jkd->tkgd', probs.astype(jnp.float32), keyvals[:, 1])
    return mixed.reshape(prefix_length, QUERY_HEADS * HEAD_WIDTH).astype(jnp.bfloat16)

def reference(mamba_x, gate_z, proj_bc, step_raw, step_bias, decay_log, skip_gain, norm_gain, state_cache, cache_slot, prefix_pages, page_table, queries, appended_memory_pair, key_value_pages):
    xs_all = mamba_x.reshape(SESSION_COUNT, SESSION_TOKENS, HM * P_SIZE)
    gates_all = gate_z.reshape(SESSION_COUNT, SESSION_TOKENS, HM * P_SIZE)
    proj_all = proj_bc.reshape(SESSION_COUNT, SESSION_TOKENS, 2, G, NS)
    raw_all = step_raw.reshape(HM, SESSION_COUNT, SESSION_TOKENS).transpose(1, 0, 2)
    asked_all = queries.reshape(SESSION_COUNT, SESSION_TOKENS, QUERY_HEADS * HEAD_WIDTH)
    fresh_tokens_all = appended_memory_pair.reshape(SESSION_COUNT, SESSION_TOKENS, 2, KEY_VALUE_HEADS, HEAD_WIDTH)

    def one_session(packed):
        values, gates, proj, raw_steps, slot, npages, table, requested, fresh_kv = packed
        start = lax.dynamic_index_in_dim(state_cache, slot.astype(jnp.int32), 0, keepdims=False)
        mixed, fresh = mamba_session(values, gates, proj, raw_steps, start, step_bias, decay_log, skip_gain, norm_gain)
        owner = (slot // S_DEV).astype(jnp.int32)
        row_index = (owner * POOLP + table).astype(jnp.int32)
        page_key_value = jnp.take(key_value_pages, row_index, axis=0).reshape(LONGEST_PAGES * PAGE_TOKENS, 2, KEY_VALUE_HEADS, HEAD_WIDTH)
        attended = attend_session(requested, fresh_kv, page_key_value, npages)
        return (mixed, fresh, attended)
    mixed, fresh, attended = lax.map(one_session, (xs_all, gates_all, proj_all, raw_all, cache_slot, prefix_pages, page_table, asked_all, fresh_tokens_all))
    return (mixed.reshape(ADDED_ITEM_TALLY, HM * P_SIZE), fresh, attended.reshape(ADDED_ITEM_TALLY, QUERY_HEADS * HEAD_WIDTH))
```

```python
import functools

import jax
import jax.numpy as jnp
from jax import lax
from jax.experimental import pallas as pl
from jax.experimental.pallas import tpu as pltpu
from jax.sharding import PartitionSpec as P

HM = 128
P_SIZE = 64
NS = 256
G = 4
HEAD_WIDTH = 128
PAGE_TOKENS = 64
EPS = 1e-05

BUCKETS = (3, 4, 5, 6, 8)
HIGHEST = lax.Precision.HIGHEST
F32 = jnp.float32
BF16 = jnp.bfloat16


def params():
    return pltpu.CompilerParams(vmem_limit_bytes=40 * 1024 * 1024)


def cost(flops, moved):
    return pl.CostEstimate(flops=flops, bytes_accessed=moved, transcendentals=0)


def swapped(block, axis, stride):
    count = lax.axis_size(axis)
    route = []
    for low in range(count):
        high = low | 1 << stride
        if high != low and high < count:
            route += [(low, high), (high, low)]
    return lax.ppermute(block, axis, route)


def exchange(block):
    return lax.all_to_all(block, "sess", split_axis=0, concat_axis=0, tiled=True)


def routing(cache_slot, page_table, me, slots):
    blocks = cache_slot.shape[0] // slots
    owner = (cache_slot // slots).reshape(blocks, slots)
    local = (cache_slot % slots).reshape(blocks, slots)
    tables = page_table.reshape(blocks, slots, page_table.shape[1])
    names = jnp.arange(blocks, dtype=jnp.int32)
    place = jnp.arange(slots, dtype=jnp.int32)

    def flag(value):
        return value.astype(jnp.int32)

    same = flag(owner[:, :, None] == owner[:, None, :])
    earlier = flag(place[None, :] < place[:, None])
    before = jnp.sum(same * earlier[None], axis=2)
    hot = flag(owner[:, :, None] == names)
    first = hot * flag(before == 0)[:, :, None]
    second = hot * flag(before == 1)[:, :, None]
    extra = jnp.sum(second, axis=1)
    lower = flag(names[None, :] < names[:, None])
    rank_owner = jnp.sum(lower[:, :, None] * extra[None, :, :], axis=1)
    rank_dest = jnp.sum(lower[None, :, :] * extra[:, None, :], axis=2)
    worst = jnp.maximum(jnp.max(jnp.sum(extra, axis=0)), jnp.max(jnp.sum(extra, axis=1)))

    most = BUCKETS[-1]
    ranks = jnp.arange(most, dtype=jnp.int32)
    mine = flag(names == me)
    mine_first = jnp.sum(first * mine, axis=2)
    mine_second = jnp.sum(second * mine, axis=2)
    direct_slot = jnp.sum(mine_first * local, axis=1)
    direct_pages = jnp.sum(mine_first[:, :, None] * tables, axis=1)
    my_rank = jnp.sum(rank_owner * mine, axis=1)
    chosen = mine_second[:, :, None] * flag(my_rank[:, None] == ranks)[:, None, :]
    excess_slot = jnp.sum(chosen * local[:, :, None], axis=(0, 1))
    excess_pages = jnp.sum(chosen[:, :, :, None] * tables[:, :, None, :], axis=(0, 1))

    taken = extra[:, :, None] * flag(rank_dest[:, :, None] == ranks)
    from_owner = jnp.sum(taken * names[None, :, None], axis=1)
    from_rank = jnp.sum(taken * rank_owner[:, :, None], axis=1)

    at = flag(names == me)
    my_owner = jnp.sum(at[:, None] * owner, axis=0)
    second_place = jnp.sum(second * place[None, :, None], axis=1)
    my_taken = jnp.sum(at[:, None, None] * taken, axis=0)
    my_second = jnp.sum(at[:, None] * second_place, axis=0)
    excess_session = jnp.sum(my_taken * my_second[:, None], axis=0)
    excess_valid = jnp.sum(my_taken, axis=0)
    return dict(
        direct_slot=direct_slot,
        direct_pages=direct_pages.reshape(-1),
        excess_slot=excess_slot,
        excess_pages=excess_pages.reshape(-1),
        from_owner=from_owner.reshape(-1),
        from_rank=from_rank.reshape(-1),
        my_owner=my_owner,
        excess_session=excess_session,
        excess_valid=excess_valid,
        worst=worst,
    )


def pick_kernel(index, source, target):
    target[...] = source[...]


def pick_states(state_cache, index):
    count = index.shape[0]
    shape = state_cache.shape[1:]
    size = 2 * shape[0] * shape[1] * shape[2]
    return pl.pallas_call(
        pick_kernel,
        grid_spec=pltpu.PrefetchScalarGridSpec(
            num_scalar_prefetch=1,
            grid=(count,),
            in_specs=[pl.BlockSpec((1,) + shape, lambda i, index: (index[i], 0, 0, 0))],
            out_specs=pl.BlockSpec((1,) + shape, lambda i, index: (i, 0, 0, 0)),
        ),
        out_shape=jax.ShapeDtypeStruct((count,) + shape, state_cache.dtype),
        compiler_params=params(),
        cost_estimate=cost(0, 2 * count * size),
        name="pick_states",
    )(index, state_cache)


def cut_kernel(index, source, target):
    target[:, 0] = source[0]


def cut_states(state_cache, index):
    count = index.shape[0]
    heads, width, depth = state_cache.shape[1:]
    return pl.pallas_call(
        cut_kernel,
        grid_spec=pltpu.PrefetchScalarGridSpec(
            num_scalar_prefetch=1,
            grid=(count,),
            in_specs=[
                pl.BlockSpec((1, heads, width, depth), lambda i, index: (index[i], 0, 0, 0))
            ],
            out_specs=pl.BlockSpec((heads, 1, width, depth), lambda i, index: (0, i, 0, 0)),
        ),
        out_shape=jax.ShapeDtypeStruct((heads, count, width, depth), state_cache.dtype),
        compiler_params=params(),
        cost_estimate=cost(0, 4 * count * heads * width * depth),
        name="cut_states",
    )(index, state_cache)


def pack_pages_kernel(blocks, count, piece, direct_pages, excess_pages, pages, target, sem):
    tokens = pages.shape[1]
    per = direct_pages.shape[0] // blocks
    kept = per * tokens

    def direct(n):
        d, m = n // per, n % per
        return pltpu.make_async_copy(
            pages.at[direct_pages[n]],
            target.at[d, pl.ds(pl.multiple_of(m * tokens, tokens), tokens)],
            sem.at[n],
        )

    def excess(n):
        i, k = n // blocks, n % blocks
        start = k * piece
        page = excess_pages[i * per + start // tokens]
        return pltpu.make_async_copy(
            pages.at[page, pl.ds(pl.multiple_of(start % tokens, piece), piece)],
            target.at[k, pl.ds(pl.multiple_of(kept + i * piece, piece), piece)],
            sem.at[blocks * per + n],
        )

    def loop(total, make, act):
        def body(n, carry):
            act(make(n))
            return carry

        lax.fori_loop(0, total, body, 0)

    loop(blocks * per, direct, lambda c: c.start())
    loop(blocks * count, excess, lambda c: c.start())
    loop(blocks * per, direct, lambda c: c.wait())
    loop(blocks * count, excess, lambda c: c.wait())


def pack_pages(pages, direct_pages, excess_pages, blocks, count):
    tokens, width = pages.shape[1:]
    per = direct_pages.shape[0] // blocks
    piece = per * tokens // blocks
    rows = per * tokens + count * piece
    smem = pl.BlockSpec(memory_space=pltpu.SMEM)
    return pl.pallas_call(
        functools.partial(pack_pages_kernel, blocks, count, piece),
        in_specs=[smem, smem, pl.BlockSpec(memory_space=pl.ANY)],
        out_specs=pl.BlockSpec(memory_space=pl.ANY),
        out_shape=jax.ShapeDtypeStruct((blocks, rows, width), pages.dtype),
        scratch_shapes=[pltpu.SemaphoreType.DMA((blocks * (per + count),))],
        compiler_params=params(),
        cost_estimate=cost(0, 4 * blocks * rows * width),
        name="pack_pages",
    )(direct_pages, excess_pages, pages)


def relay_kernel(blocks, count, most, kept, piece, owner, rank, states, pages, target, sem):
    width = states.shape[2]

    def state_copy(n):
        d, i = n // count, n % count
        at = d * most + i
        return pltpu.make_async_copy(
            states.at[owner[at], rank[at]], target.at[d, i, pl.ds(0, width)], sem.at[2 * n]
        )

    def page_copy(n):
        d, i = n // count, n % count
        at = d * most + i
        start = pl.multiple_of(kept + rank[at] * piece, piece)
        return pltpu.make_async_copy(
            pages.at[owner[at], pl.ds(start, piece)],
            target.at[d, i, pl.ds(width, piece)],
            sem.at[2 * n + 1],
        )

    def start(n, carry):
        state_copy(n).start()
        page_copy(n).start()
        return carry

    def wait(n, carry):
        state_copy(n).wait()
        page_copy(n).wait()
        return carry

    lax.fori_loop(0, blocks * count, start, 0)
    lax.fori_loop(0, blocks * count, wait, 0)


def relay(states, pages, owner, rank, count, kept):
    blocks, _, width, depth = states.shape
    piece = (pages.shape[1] - kept) // count
    smem = pl.BlockSpec(memory_space=pltpu.SMEM)
    hbm = pl.BlockSpec(memory_space=pl.ANY)
    shape = (blocks, count, width + piece, depth)
    return pl.pallas_call(
        functools.partial(
            relay_kernel, blocks, count, owner.shape[0] // blocks, kept, piece
        ),
        in_specs=[smem, smem, hbm, hbm],
        out_specs=hbm,
        out_shape=jax.ShapeDtypeStruct(shape, states.dtype),
        scratch_shapes=[pltpu.SemaphoreType.DMA((2 * blocks * count,))],
        compiler_params=params(),
        cost_estimate=cost(0, 4 * blocks * count * (width + piece) * depth),
        name="relay",
    )(owner, rank, states, pages)


def dot(a, b, dims, precision=None):
    return lax.dot_general(
        a, b, ((dims[:1], dims[1:]), ((), ())), precision=precision, preferred_element_type=F32
    )


def spread_matrix(heads, lanes):
    row = lax.broadcasted_iota(jnp.int32, (heads, heads * lanes), 0)
    column = lax.broadcasted_iota(jnp.int32, (heads, heads * lanes), 1)
    return (row == column // lanes).astype(F32)


def spread(columns, lanes):
    return dot(columns, spread_matrix(columns.shape[1], lanes), (1, 0), HIGHEST)


def before_kernel(x_ref, b_ref, c_ref, cumul_ref, tail_ref, row_ref, skip_ref, base, scaled):
    heads = cumul_ref.shape[2]
    tokens = x_ref.shape[0]
    quad = 4
    x = x_ref[...]
    inner = dot(c_ref[...], b_ref[...], (1, 1))
    at_t = spread(cumul_ref[0], tokens)
    row = lax.broadcasted_iota(jnp.int32, at_t.shape, 0)
    column = lax.broadcasted_iota(jnp.int32, at_t.shape, 1)
    causal = row >= column % tokens
    gap = at_t - row_ref[0, 0:1]
    decay = jnp.where(causal, jnp.exp(jnp.where(causal, gap, 0.0)), 0.0)
    inner = jnp.concatenate([inner] * heads, axis=1)
    weights = (inner * decay * row_ref[0, 1:2]).astype(BF16)
    own_row = lax.broadcasted_iota(jnp.int32, (quad * tokens, quad * P_SIZE), 0) // tokens
    own_column = lax.broadcasted_iota(jnp.int32, (quad * tokens, quad * P_SIZE), 1) // P_SIZE
    own = own_row == own_column
    for q in range(heads // quad):
        lanes = slice(q * quad * P_SIZE, (q + 1) * quad * P_SIZE)
        values = x[:, lanes].astype(F32)
        stacked = jnp.where(own, jnp.concatenate([values] * quad, axis=0), 0.0).astype(BF16)
        part = weights[:, q * quad * tokens : (q + 1) * quad * tokens]
        base[:, lanes] = dot(part, stacked, (1, 0)) + skip_ref[:, lanes] * values
    scaled[...] = (x.astype(F32) * spread(tail_ref[0], P_SIZE)).astype(BF16)


def mamba_before(x, b, c, cumul, tail, rows, skip):
    total, width = x.shape
    slots, tokens, heads = cumul.shape
    per = lambda shape: pl.BlockSpec(shape, lambda s: (s,) + (0,) * (len(shape) - 1))
    return pl.pallas_call(
        before_kernel,
        grid=(slots,),
        in_specs=[
            per((tokens, width)),
            per((tokens, NS)),
            per((tokens, NS)),
            per((1, tokens, heads)),
            per((1, tokens, heads)),
            per((1, 2, heads * tokens)),
            pl.BlockSpec((1, width), lambda s: (0, 0)),
        ],
        out_specs=[per((tokens, width)), per((tokens, width))],
        out_shape=[
            jax.ShapeDtypeStruct((total, width), F32),
            jax.ShapeDtypeStruct((total, width), BF16),
        ],
        compiler_params=params(),
        cost_estimate=cost(10**9, 20 * 2**20),
        name="mamba_before",
    )(x, b, c, cumul, tail, rows, skip)


def mamba_step(state, base, c, b, scaled, cumul, gate, carry, gated, squares, fresh):
    heads = state.shape[0]
    carried = dot(c, state.reshape(heads * P_SIZE, NS), (1, 1))
    out = base + carried * spread(jnp.exp(cumul), P_SIZE)
    gate = gate.astype(F32)
    value = out * (gate / (1.0 + jnp.exp(-gate)))
    gated[...] = value
    ones = jnp.ones((8, value.shape[1]), F32)
    squares[0] = dot(ones, value * value, (1, 1), HIGHEST)[0:1]
    local = dot(scaled, b, (0, 0))
    for h in range(heads):
        rows = slice(h * P_SIZE, (h + 1) * P_SIZE)
        fresh[0, h] = (carry[h : h + 1] * state[h].astype(F32) + local[rows]).astype(BF16)


def attend_step(pages, queries, new, prefix, out):
    kept = pages.shape[0]
    tokens = queries.shape[0]
    heads = queries.shape[1] // HEAD_WIDTH
    q = jnp.concatenate(
        [queries[:, g * HEAD_WIDTH : (g + 1) * HEAD_WIDTH] for g in range(heads)], axis=0
    )
    factor = HEAD_WIDTH ** (-0.5)
    old_scores = dot(q, pages[:, :HEAD_WIDTH], (1, 1)) * factor
    new_scores = dot(q, new[:, :HEAD_WIDTH], (1, 1)) * factor
    column = lax.broadcasted_iota(jnp.int32, old_scores.shape, 1)
    old_scores = jnp.where(column < prefix * PAGE_TOKENS, old_scores, -jnp.inf)
    row = lax.broadcasted_iota(jnp.int32, new_scores.shape, 0) % tokens
    column = lax.broadcasted_iota(jnp.int32, new_scores.shape, 1)
    new_scores = jnp.where(column <= row, new_scores, -jnp.inf)
    peak = jnp.maximum(
        jnp.max(old_scores, axis=1, keepdims=True), jnp.max(new_scores, axis=1, keepdims=True)
    )
    old_expo = jnp.exp(old_scores - peak)
    new_expo = jnp.exp(new_scores - peak)
    total = jnp.sum(old_expo, axis=1, keepdims=True) + jnp.sum(new_expo, axis=1, keepdims=True)
    old_probs = (old_expo / total).astype(BF16)
    new_probs = (new_expo / total).astype(BF16)
    mixed = dot(old_probs, pages[:, HEAD_WIDTH:], (1, 0)) + dot(
        new_probs, new[:, HEAD_WIDTH:], (1, 0)
    )
    for g in range(heads):
        out[:, g * HEAD_WIDTH : (g + 1) * HEAD_WIDTH] = mixed[
            g * tokens : (g + 1) * tokens
        ].astype(BF16)


def attend_kernel(owner, prefix, pages, queries, new, out):
    s = pl.program_id(0)
    attend_step(pages[0], queries[...], new[...], prefix[s], out)


def attend_direct(owner, prefix, pages, queries, new, kept):
    slots = owner.shape[0]
    total, width = queries.shape
    tokens = total // slots
    own = lambda s, owner, prefix: (s, 0)
    return pl.pallas_call(
        attend_kernel,
        grid_spec=pltpu.PrefetchScalarGridSpec(
            num_scalar_prefetch=2,
            grid=(slots,),
            in_specs=[
                pl.BlockSpec(
                    (1, kept, pages.shape[2]), lambda s, owner, prefix: (owner[s], 0, 0)
                ),
                pl.BlockSpec((tokens, width), own),
                pl.BlockSpec((tokens, new.shape[1]), own),
            ],
            out_specs=pl.BlockSpec((tokens, width), own),
        ),
        out_shape=jax.ShapeDtypeStruct((total, width), BF16),
        compiler_params=params(),
        cost_estimate=cost(10**9, 8 * 2**20),
        name="attend_direct",
    )(owner, prefix, pages, queries, new)


def after_kernel(owner, state, base, c, b, scaled, cumul, gate, carry, gated, squares, fresh):
    mamba_step(
        state[0], base[...], c[...], b[...], scaled[...], cumul[0], gate[...], carry[0],
        gated, squares, fresh,
    )


def mamba_direct(owner, states, base, c, b, scaled, cumul, gate, carry):
    slots, tokens, heads = cumul.shape
    total, width = base.shape
    shape = states.shape[1:]
    own2 = lambda s, owner: (s, 0)
    own3 = lambda s, owner: (s, 0, 0)
    return pl.pallas_call(
        after_kernel,
        grid_spec=pltpu.PrefetchScalarGridSpec(
            num_scalar_prefetch=1,
            grid=(slots,),
            in_specs=[
                pl.BlockSpec((1,) + shape, lambda s, owner: (owner[s], 0, 0, 0)),
                pl.BlockSpec((tokens, width), own2),
                pl.BlockSpec((tokens, NS), own2),
                pl.BlockSpec((tokens, NS), own2),
                pl.BlockSpec((tokens, width), own2),
                pl.BlockSpec((1, tokens, heads), own3),
                pl.BlockSpec((tokens, width), own2),
                pl.BlockSpec((1, heads, NS), own3),
            ],
            out_specs=[
                pl.BlockSpec((tokens, width), own2),
                pl.BlockSpec((1, 1, tokens), own3),
                pl.BlockSpec((1,) + shape, lambda s, owner: (s, 0, 0, 0)),
            ],
        ),
        out_shape=[
            jax.ShapeDtypeStruct((total, width), F32),
            jax.ShapeDtypeStruct((slots, 1, tokens), F32),
            jax.ShapeDtypeStruct((slots,) + shape, BF16),
        ],
        compiler_params=params(),
        cost_estimate=cost(10**9, 25 * 2**20),
        name="mamba_direct",
    )(owner, states, base, c, b, scaled, cumul, gate, carry)


def excess_kernel(
    session, valid, prefix,
    block, base, c, b, scaled, cumul, gate, carry, queries, new,
    gated_in, squares_in, fresh_in, out_in,
    gated, squares, fresh, out,
):
    i = pl.program_id(0)
    width = fresh.shape[2]
    heads = fresh.shape[1]

    @pl.when(valid[i] > 0)
    def _():
        mamba_step(
            block[:, 0, :width], base[...], c[...], b[...], scaled[...], cumul[0], gate[...],
            carry[0], gated, squares, fresh,
        )
        pages = block[:, 0, width:]
        pages = pages.reshape(heads * pages.shape[1], pages.shape[2])
        attend_step(pages, queries[...], new[...], prefix[session[i]], out)

    @pl.when(valid[i] == 0)
    def _():
        gated[...] = gated_in[...]
        squares[...] = squares_in[...]
        fresh[...] = fresh_in[...]
        out[...] = out_in[...]


def finish_excess(
    session, valid, prefix, items, base, c, b, scaled, cumul, gate, carry, queries, new,
    gated, squares, fresh, out,
):
    count = items.shape[1]
    slots, tokens, heads = cumul.shape
    total, width = base.shape
    shape = fresh.shape[1:]

    def own(block):
        rest = (0,) * (len(block) - 1)
        return pl.BlockSpec(block, lambda i, session, valid, prefix: (session[i],) + rest)

    results = [
        own((tokens, width)),
        own((1, 1, tokens)),
        own((1,) + shape),
        own((tokens, width)),
    ]
    return pl.pallas_call(
        excess_kernel,
        grid_spec=pltpu.PrefetchScalarGridSpec(
            num_scalar_prefetch=3,
            grid=(count,),
            in_specs=[
                pl.BlockSpec(
                    (heads, 1) + items.shape[2:],
                    lambda i, session, valid, prefix: (0, i, 0, 0),
                ),
                own((tokens, width)),
                own((tokens, NS)),
                own((tokens, NS)),
                own((tokens, width)),
                own((1, tokens, heads)),
                own((tokens, width)),
                own((1, heads, NS)),
                own((tokens, width)),
                own((tokens, new.shape[1])),
            ]
            + results,
            out_specs=results,
        ),
        out_shape=[
            jax.ShapeDtypeStruct(a.shape, a.dtype) for a in (gated, squares, fresh, out)
        ],
        input_output_aliases={13: 0, 14: 1, 15: 2, 16: 3},
        compiler_params=params(),
        cost_estimate=cost(10**8, 8 * 2**20),
        name="finish_excess",
    )(
        session, valid, prefix, items, base, c, b, scaled, cumul, gate, carry, queries, new,
        gated, squares, fresh, out,
    )


def shards(
    mamba_x,
    gate_z,
    proj_bc,
    step_raw,
    step_bias,
    decay_log,
    skip_gain,
    norm_gain,
    state_cache,
    cache_slot,
    prefix_pages,
    page_table,
    queries,
    appended_memory_pair,
    key_value_pages,
):
    slots, heads = state_cache.shape[:2]
    blocks = cache_slot.shape[0] // slots
    total = mamba_x.shape[0]
    tokens = total // slots
    kept = page_table.shape[1] * PAGE_TOKENS
    tables = routing(cache_slot, page_table, lax.axis_index("sess"), slots)

    def run(count, _):
        sent = cut_states(state_cache, tables["excess_slot"][:count])
        relayed_states = exchange(sent)

        pages = key_value_pages.reshape(key_value_pages.shape[:2] + (2 * HEAD_WIDTH,))
        per = page_table.shape[1]
        got_pages = exchange(
            pack_pages(
                pages, tables["direct_pages"], tables["excess_pages"][: count * per], blocks, count
            )
        )
        got_states = exchange(pick_states(state_cache, tables["direct_slot"]))
        items = exchange(
            relay(
                relayed_states, got_pages, tables["from_owner"], tables["from_rank"], count, kept
            )
        )

        group = lax.axis_index("mp") * heads // (HM // G)
        both = lax.dynamic_index_in_dim(proj_bc, group, axis=2, keepdims=False)
        b, c = both[:, 0], both[:, 1]
        delta = jax.nn.softplus(step_raw + step_bias[:, None]).reshape(heads, slots, tokens)
        falloff = -jnp.exp(decay_log)[:, None, None] * delta
        position = jnp.arange(tokens)
        lower = (position[:, None] >= position[None, :]).astype(F32)
        cumul = jnp.einsum("hsu,tu->hst", falloff, lower, precision=HIGHEST)
        last = cumul[:, :, tokens - 1 :]
        tail = (jnp.exp(last - cumul) * delta).transpose(1, 2, 0)
        carry = jnp.exp(last[:, :, 0]).T[:, :, None]
        carry = jnp.broadcast_to(carry, (slots, heads, NS))
        rows = jnp.stack([cumul, delta], axis=0).transpose(2, 0, 1, 3)
        rows = rows.reshape(slots, 2, heads * tokens)
        cumul = cumul.transpose(1, 2, 0)
        skip = jnp.repeat(skip_gain, P_SIZE)[None, :]

        base, scaled = mamba_before(mamba_x, b, c, cumul, tail, rows, skip)
        new = appended_memory_pair.reshape(total, 2 * HEAD_WIDTH)
        out = attend_direct(tables["my_owner"], prefix_pages, got_pages, queries, new, kept)
        gated, squares, fresh = mamba_direct(
            tables["my_owner"], got_states, base, c, b, scaled, cumul, gate_z, carry
        )
        gated, squares, fresh, out = finish_excess(
            tables["excess_session"][:count], tables["excess_valid"][:count], prefix_pages,
            items, base, c, b, scaled, cumul, gate_z, carry, queries, new,
            gated, squares, fresh, out,
        )
        squares = squares.reshape(total)
        squares = squares + swapped(squares, "mp", 0)
        scale = lax.rsqrt(squares / (HM // G * P_SIZE) + EPS)
        mixed = (gated * scale[:, None] * norm_gain[None, :]).astype(BF16)
        return mixed, fresh, out

    limits = jnp.array(BUCKETS[:-1], jnp.int32)
    choice = jnp.sum((tables["worst"] > limits).astype(jnp.int32))
    return lax.switch(choice, [functools.partial(run, count) for count in BUCKETS], 0)


def solution(mesh):
    return jax.shard_map(
        shards,
        mesh=mesh,
        in_specs=(
            P("sess", "mp"),
            P("sess", "mp"),
            P("sess", None, None, None),
            P("mp", "sess"),
            P("mp"),
            P("mp"),
            P("mp"),
            P("mp"),
            P("sess", "mp", None, None),
            P(),
            P("sess"),
            P(),
            P("sess", "mp"),
            P("sess", None, "mp", None),
            P("sess", None, None, "mp", None),
        ),
        out_specs=(P("sess", "mp"), P("sess", "mp", None, None), P("sess", "mp")),
        check_vma=False,
    )
```

```python
import functools

import jax
import jax.numpy as jnp
from jax import lax
from jax.experimental import pallas as pl
from jax.experimental.pallas import tpu as pltpu
from jax.sharding import PartitionSpec as P

HM = 128
P_SIZE = 64
NS = 256
G = 4
HEAD_WIDTH = 128
CAP = 2
PAGE_TOKENS = 64
EPS = 1e-05

STEPS = (10, 11, 12, 13, 14)
DELAY = 1
SIDE = 4
HIGHEST = lax.Precision.HIGHEST
F32 = jnp.float32
BF16 = jnp.bfloat16


def params():
    return pltpu.CompilerParams(vmem_limit_bytes=56 * 1024 * 1024)


def cost(flops, moved):
    return pl.CostEstimate(flops=flops, bytes_accessed=moved, transcendentals=0)


def swapped(block, axis, stride):
    count = lax.axis_size(axis)
    route = []
    for low in range(count):
        high = low | 1 << stride
        if high != low and high < count:
            route += [(low, high), (high, low)]
    return lax.ppermute(block, axis, route)


def send_plan(cache_slot, page_table, sender, slots):
    blocks = cache_slot.shape[0] // slots
    owner_grid = (cache_slot // slots).reshape(blocks, slots)
    local_grid = (cache_slot % slots).reshape(blocks, slots)
    mine = (owner_grid == sender).astype(jnp.int32)
    before = jnp.cumsum(mine, axis=1) - mine
    which = jnp.arange(CAP, dtype=jnp.int32)
    match = mine[:, None, :] * (before[:, None, :] == which[None, :, None]).astype(jnp.int32)
    send_slots = jnp.sum(match * local_grid[:, None, :], axis=2)
    tables = page_table.reshape(blocks, 1, slots, page_table.shape[1])
    send_pages = jnp.sum(match[:, :, :, None] * tables, axis=2)
    return (send_slots, send_pages)


def pick_plan(cache_slot, receiver, slots):
    own_row = lax.dynamic_slice_in_dim(cache_slot, receiver * slots, slots) // slots
    same_owner = (own_row[:, None] == own_row[None, :]).astype(jnp.int32)
    position = jnp.arange(slots)
    earlier = (position[None, :] < position[:, None]).astype(jnp.int32)
    ranked = jnp.sum(same_owner * earlier, axis=1)
    return own_row * CAP + ranked


def group_total(squares):
    total = squares
    total = total + swapped(total, "mp", 0)
    return total


def mamba_part(
    mamba_x, gate_z, proj_bc, step_raw, step_bias, decay_log, skip_gain, norm_gain, start_state
):
    slots = start_state.shape[0]
    heads = step_raw.shape[0]
    prefix_length = mamba_x.shape[0] // slots
    group = lax.axis_index("mp") * heads // (HM // G)
    both = lax.dynamic_index_in_dim(proj_bc, group, axis=2, keepdims=False)
    inputs_b = both[:, 0].reshape(slots, prefix_length, NS)
    inputs_c = both[:, 1].reshape(slots, prefix_length, NS)
    delta = jax.nn.softplus(step_raw + step_bias[:, None]).reshape(heads, slots, prefix_length)
    falloff_factor = -jnp.exp(decay_log)[:, None, None] * delta
    position = jnp.arange(prefix_length)
    lower = (position[:, None] >= position[None, :]).astype(jnp.float32)
    cumul = jnp.einsum("hsu,tu->hst", falloff_factor, lower, precision=lax.Precision.HIGHEST)
    causal = lower > 0
    spread = cumul[:, :, :, None] - cumul[:, :, None, :]
    decay = jnp.where(causal, jnp.exp(jnp.where(causal, spread, 0.0)), 0.0)
    inner = jnp.einsum("stn,sun->stu", inputs_c, inputs_b, preferred_element_type=jnp.float32)
    weights = (inner[None] * decay * delta[:, :, None, :]).astype(jnp.bfloat16)
    values = mamba_x.reshape(slots, prefix_length, heads, P_SIZE)
    intra = jnp.einsum("hstu,suhp->sthp", weights, values, preferred_element_type=jnp.float32)
    carried = jnp.einsum(
        "stn,shpn->sthp", inputs_c, start_state, preferred_element_type=jnp.float32
    )
    expansion_factor = jnp.exp(cumul).transpose(1, 2, 0)[:, :, :, None]
    output = (
        intra
        + carried * expansion_factor
        + skip_gain[None, None, :, None] * values.astype(jnp.float32)
    )
    gates = gate_z.reshape(slots, prefix_length, heads, P_SIZE).astype(jnp.float32)
    gated = output * jax.nn.silu(gates)
    squares = jnp.sum(gated * gated, axis=(2, 3)).reshape(slots * prefix_length)
    total = group_total(squares)
    scale = lax.rsqrt(total / (HM // G * P_SIZE) + EPS)
    normed = (
        gated.reshape(slots * prefix_length, heads * P_SIZE) * scale[:, None] * norm_gain[None, :]
    )
    last_cumul = cumul[:, :, prefix_length - 1 :]
    tail = jnp.exp(last_cumul - cumul) * delta
    scaled = (values.astype(jnp.float32) * tail.transpose(1, 2, 0)[:, :, :, None]).astype(
        jnp.bfloat16
    )
    local = jnp.einsum("suhp,sun->shpn", scaled, inputs_b, preferred_element_type=jnp.float32)
    carry_decay = jnp.exp(last_cumul[:, :, 0]).T[:, :, None, None]
    fresh = carry_decay * start_state.astype(jnp.float32) + local
    return (normed.astype(jnp.bfloat16), fresh.astype(jnp.bfloat16))


def attend(queries, appended_memory_pair, prefix_kv, prefix_pages):
    slots = prefix_pages.shape[0]
    prefix_length = queries.shape[0] // slots
    kv_heads = appended_memory_pair.shape[2]
    grouped = queries.shape[1] // (kv_heads * HEAD_WIDTH)
    fresh_kv = appended_memory_pair.reshape(slots, prefix_length, 2, kv_heads, HEAD_WIDTH)
    keyvals = jnp.concatenate([prefix_kv, fresh_kv], axis=1)
    kept = prefix_kv.shape[1]
    requested = queries.reshape(slots, prefix_length, kv_heads, grouped, HEAD_WIDTH)
    scores = jnp.einsum(
        "stkgd,sjkd->skgtj", requested, keyvals[:, :, 0], preferred_element_type=jnp.float32
    ) * HEAD_WIDTH ** (-0.5)
    column = jnp.arange(kept + prefix_length)
    row_pos = jnp.arange(prefix_length)
    limit = prefix_pages * PAGE_TOKENS
    valid_prefix = column[None, :] < limit[:, None]
    valid_new = column[None, :] - kept <= row_pos[:, None]
    valid = jnp.where(column[None, None, :] < kept, valid_prefix[:, None, :], valid_new[None, :, :])
    scores = jnp.where(valid[:, None, None], scores, -jnp.inf)
    peak = jnp.max(scores, axis=-1, keepdims=True)
    expo = jnp.exp(scores - peak)
    probs = (expo / jnp.sum(expo, axis=-1, keepdims=True)).astype(jnp.bfloat16)
    mixed = jnp.einsum(
        "skgtj,sjkd->stkgd", probs, keyvals[:, :, 1], preferred_element_type=jnp.float32
    )
    return mixed.reshape(slots * prefix_length, kv_heads * grouped * HEAD_WIDTH).astype(
        jnp.bfloat16
    )


def padded(
    mamba_x,
    gate_z,
    proj_bc,
    step_raw,
    step_bias,
    decay_log,
    skip_gain,
    norm_gain,
    state_cache,
    cache_slot,
    prefix_pages,
    page_table,
    queries,
    appended_memory_pair,
    key_value_pages,
):
    slots = state_cache.shape[0]
    device_here = lax.axis_index("sess")
    send_slots, send_pages = send_plan(cache_slot, page_table, device_here, slots)
    picked = pick_plan(cache_slot, device_here, slots)
    state_send = jnp.take(state_cache, send_slots.reshape(-1), axis=0).reshape(
        send_slots.shape + state_cache.shape[1:]
    )
    page_send = jnp.take(key_value_pages, send_pages.reshape(-1), axis=0).reshape(
        send_slots.shape
        + (send_pages.shape[2] * key_value_pages.shape[1],)
        + key_value_pages.shape[2:]
    )
    got_states, got_pages = (
        lax.all_to_all(state_send, "sess", split_axis=0, concat_axis=0, tiled=True),
        lax.all_to_all(page_send, "sess", split_axis=0, concat_axis=0, tiled=True),
    )
    start_state = jnp.take(got_states.reshape((-1,) + state_cache.shape[1:]), picked, axis=0)
    mixed, fresh = mamba_part(
        mamba_x, gate_z, proj_bc, step_raw, step_bias, decay_log, skip_gain, norm_gain, start_state
    )
    prefix_kv = jnp.take(got_pages.reshape((-1,) + page_send.shape[2:]), picked, axis=0)
    attended = attend(queries, appended_memory_pair, prefix_kv, prefix_pages)
    return (mixed, fresh, attended)


def dot(a, b, dims, precision=None):
    return lax.dot_general(
        a, b, ((dims[:1], dims[1:]), ((), ())), precision=precision, preferred_element_type=F32
    )


def spread_matrix(heads, lanes):
    row = lax.broadcasted_iota(jnp.int32, (heads, heads * lanes), 0)
    column = lax.broadcasted_iota(jnp.int32, (heads, heads * lanes), 1)
    return (row == column // lanes).astype(F32)


def spread(columns, lanes):
    return dot(columns, spread_matrix(columns.shape[1], lanes), (1, 0), HIGHEST)


def before_kernel(x_ref, b_ref, c_ref, cumul_ref, tail_ref, row_ref, skip_ref, base, scaled):
    heads = cumul_ref.shape[2]
    tokens = x_ref.shape[0]
    quad = 4
    x = x_ref[...]
    inner = dot(c_ref[...], b_ref[...], (1, 1))
    at_t = spread(cumul_ref[0], tokens)
    row = lax.broadcasted_iota(jnp.int32, at_t.shape, 0)
    column = lax.broadcasted_iota(jnp.int32, at_t.shape, 1)
    causal = row >= column % tokens
    gap = at_t - row_ref[0, 0:1]
    decay = jnp.where(causal, jnp.exp(jnp.where(causal, gap, 0.0)), 0.0)
    inner = jnp.concatenate([inner] * heads, axis=1)
    weights = (inner * decay * row_ref[0, 1:2]).astype(BF16)
    own_row = lax.broadcasted_iota(jnp.int32, (quad * tokens, quad * P_SIZE), 0) // tokens
    own_column = lax.broadcasted_iota(jnp.int32, (quad * tokens, quad * P_SIZE), 1) // P_SIZE
    own = own_row == own_column
    for q in range(heads // quad):
        lanes = slice(q * quad * P_SIZE, (q + 1) * quad * P_SIZE)
        values = x[:, lanes].astype(F32)
        stacked = jnp.where(own, jnp.concatenate([values] * quad, axis=0), 0.0).astype(BF16)
        part = weights[:, q * quad * tokens : (q + 1) * quad * tokens]
        base[:, lanes] = dot(part, stacked, (1, 0)) + skip_ref[:, lanes] * values
    scaled[...] = (x.astype(F32) * spread(tail_ref[0], P_SIZE)).astype(BF16)


def mamba_before(x, b, c, cumul, tail, rows, skip):
    total, width = x.shape
    slots, tokens, heads = cumul.shape
    per = lambda shape: pl.BlockSpec(shape, lambda s: (s,) + (0,) * (len(shape) - 1))
    return pl.pallas_call(
        before_kernel,
        grid=(slots,),
        in_specs=[
            per((tokens, width)),
            per((tokens, NS)),
            per((tokens, NS)),
            per((1, tokens, heads)),
            per((1, tokens, heads)),
            per((1, 2, heads * tokens)),
            pl.BlockSpec((1, width), lambda s: (0, 0)),
        ],
        out_specs=[per((tokens, width)), per((tokens, width))],
        out_shape=[
            jax.ShapeDtypeStruct((total, width), F32),
            jax.ShapeDtypeStruct((total, width), BF16),
        ],
        compiler_params=params(),
        cost_estimate=cost(10**9, 20 * 2**20),
        name="mamba_before",
    )(x, b, c, cumul, tail, rows, skip)


def mamba_step(state, base, c, b, scaled, cumul, gate, carry, gated, squares, fresh):
    heads = state.shape[0]
    carried = dot(c, state.reshape(heads * P_SIZE, NS), (1, 1))
    out = base + carried * spread(jnp.exp(cumul), P_SIZE)
    gate = gate.astype(F32)
    value = out * (gate / (1.0 + jnp.exp(-gate)))
    gated[...] = value
    ones = jnp.ones((8, value.shape[1]), F32)
    squares[0] = dot(ones, value * value, (1, 1), HIGHEST)[0:1]
    local = dot(scaled, b, (0, 0))
    for h in range(heads):
        rows = slice(h * P_SIZE, (h + 1) * P_SIZE)
        fresh[0, h] = (carry[h : h + 1] * state[h].astype(F32) + local[rows]).astype(BF16)


def attend_step(pages, queries, new, prefix, out):
    kept = pages.shape[0]
    tokens = queries.shape[0]
    heads = queries.shape[1] // HEAD_WIDTH
    q = jnp.concatenate(
        [queries[:, g * HEAD_WIDTH : (g + 1) * HEAD_WIDTH] for g in range(heads)], axis=0
    )
    factor = HEAD_WIDTH ** (-0.5)
    old_scores = dot(q, pages[:, :HEAD_WIDTH], (1, 1)) * factor
    new_scores = dot(q, new[:, :HEAD_WIDTH], (1, 1)) * factor
    column = lax.broadcasted_iota(jnp.int32, old_scores.shape, 1)
    old_scores = jnp.where(column < prefix * PAGE_TOKENS, old_scores, -jnp.inf)
    row = lax.broadcasted_iota(jnp.int32, new_scores.shape, 0) % tokens
    column = lax.broadcasted_iota(jnp.int32, new_scores.shape, 1)
    new_scores = jnp.where(column <= row, new_scores, -jnp.inf)
    peak = jnp.maximum(
        jnp.max(old_scores, axis=1, keepdims=True), jnp.max(new_scores, axis=1, keepdims=True)
    )
    old_expo = jnp.exp(old_scores - peak)
    new_expo = jnp.exp(new_scores - peak)
    total = jnp.sum(old_expo, axis=1, keepdims=True) + jnp.sum(new_expo, axis=1, keepdims=True)
    old_probs = (old_expo / total).astype(BF16)
    new_probs = (new_expo / total).astype(BF16)
    mixed = dot(old_probs, pages[:, HEAD_WIDTH:], (1, 0)) + dot(
        new_probs, new[:, HEAD_WIDTH:], (1, 0)
    )
    for g in range(heads):
        out[:, g * HEAD_WIDTH : (g + 1) * HEAD_WIDTH] = mixed[
            g * tokens : (g + 1) * tokens
        ].astype(BF16)


def schedule_kernel(most, dest_ref, table_ref, final_ref):
    dest = dest_ref[...]
    items = dest.shape[1]
    nodes = table_ref.shape[0]
    lane = lax.broadcasted_iota(jnp.int32, (1, items), 1)
    node = lax.broadcasted_iota(jnp.int32, (nodes, items), 0)
    slot = lax.broadcasted_iota(jnp.int32, table_ref.shape, 1)
    per = items // nodes
    yd, xd = dest // SIDE, dest % SIDE

    def step(t, carry):
        y, x, code, ready, table = carry
        ry, rx = (yd - y) & (SIDE - 1), (xd - x) & (SIDE - 1)
        want = [
            (rx == 1) | (rx == 2),
            (rx == 3) | (rx == 2),
            (ry == 1) | (ry == 2),
            (ry == 3) | (ry == 2),
        ]
        want = [w.astype(F32) for w in want]
        ways = want[0] + want[1] + want[2] + want[3]
        share = jnp.where(ways > 0.0, 12.0 / jnp.maximum(ways, 1.0), 0.0)
        left = (jnp.minimum(rx, SIDE - rx) + jnp.minimum(ry, SIDE - ry)).astype(F32)
        here = ((node == y * SIDE + x) & (ready <= t)).astype(F32)
        demand = [jnp.sum(here * (w * share), axis=1, keepdims=True) for w in want]
        pull = sum(w * d for w, d in zip(want, demand))
        rank = []
        for a in range(4):
            lower = 0.0
            for b in range(4):
                if b != a:
                    under = demand[b] <= demand[a] if b < a else demand[b] < demand[a]
                    lower = lower + under.astype(F32)
            rank.append(lower)
        free = here
        code_f = code.astype(F32)
        moves = [jnp.zeros((nodes, items), F32) for _ in range(4)]
        for r in range(4):
            turn = [(k == float(r)).astype(F32) for k in rank]
            wanted = sum(w * u for w, u in zip(want, turn)) * free
            own = sum(d * u for d, u in zip(demand, turn))
            value = left * 192.0 + (pull - own)
            key = jnp.where(wanted > 0.0, jnp.floor(value + 0.5) * 128.0 + (127.0 - code_f), -1.0)
            best = jnp.max(key, axis=1, keepdims=True)
            taken = ((key == best) & (best >= 0.0)).astype(F32)
            free = free * (1.0 - taken)
            picked = 127 - (best.astype(jnp.int32) & 127)
            for d in range(4):
                moves[d] = moves[d] + taken * turn[d]
                here_now = (slot == t * 4 + d) & (turn[d] > 0.0) & (best >= 0.0)
                table = jnp.where(here_now, picked, table)
        gone = [jnp.sum(m, axis=0, keepdims=True).astype(jnp.int32) for m in moves]
        x = (x + gone[0] - gone[1]) & (SIDE - 1)
        y = (y + gone[2] - gone[3]) & (SIDE - 1)
        for d in range(4):
            code = jnp.where(gone[d] > 0, per + t * 4 + d, code)
        ready = jnp.where(gone[0] + gone[1] + gone[2] + gone[3] > 0, t + 1 + DELAY, ready)
        return y, x, code, ready, table

    at = lane // per
    zero = jnp.zeros((1, items), jnp.int32)
    table = jnp.full(table_ref.shape, -1, jnp.int32)
    y, x, code, _, table = lax.fori_loop(
        0, most, step, (at // SIDE, at % SIDE, lane % per, zero, table)
    )
    table_ref[...] = table
    final_ref[...] = jnp.where(y * SIDE + x == dest, code, 127)


def schedule(dest, nodes):
    return pl.pallas_call(
        functools.partial(schedule_kernel, STEPS[-1]),
        out_shape=[
            jax.ShapeDtypeStruct((nodes, 128), jnp.int32),
            jax.ShapeDtypeStruct(dest.shape, jnp.int32),
        ],
        compiler_params=params(),
        cost_estimate=cost(10**7, 2**20),
        name="schedule",
    )(dest)


def item_copies(code, pages, state, pool, received, target, sem):
    local = state.shape[0]
    rows = state.shape[1]
    per = pages.shape[0] // local
    tokens = pool.shape[1]

    @pl.when((code >= 0) & (code < local))
    def _():
        pltpu.make_async_copy(state.at[code], target.at[pl.ds(0, rows)], sem).start()
        for m in range(per):
            pltpu.make_async_copy(
                pool.at[pages[code * per + m]],
                target.at[pl.ds(rows + m * tokens, tokens)],
                sem,
            ).start()

    for b, source in enumerate(received):

        @pl.when(code == local + b)
        def _(source=source):
            pltpu.make_async_copy(source, target, sem).start()


def gather_kernel(t, codes, pages, state, pool, *refs):
    received, targets, sem = refs[:-5], refs[-5:-1], refs[-1]
    for d in range(4):
        item_copies(codes[4 * t + d], pages, state, pool, received, targets[d], sem.at[d])
    for d in range(4):

        @pl.when(codes[4 * t + d] >= 0)
        def _(d=d):
            pltpu.make_async_copy(targets[d], targets[d], sem.at[d]).wait()


def gather(t, codes, pages, state, pool, received):
    rows = state.shape[1] + pages.shape[0] // state.shape[0] * pool.shape[1]
    smem = pl.BlockSpec(memory_space=pltpu.SMEM)
    hbm = pl.BlockSpec(memory_space=pltpu.HBM)
    out = jax.ShapeDtypeStruct((rows, state.shape[2]), state.dtype)
    return pl.pallas_call(
        functools.partial(gather_kernel, t),
        in_specs=[smem, smem] + [hbm] * (2 + len(received)),
        out_specs=[hbm] * 4,
        out_shape=[out] * 4,
        scratch_shapes=[pltpu.SemaphoreType.DMA((4,))],
        compiler_params=params(),
        cost_estimate=cost(0, 16 * rows * state.shape[2]),
        name="gather_step",
    )(codes, pages, state, pool, *received)


def shift(block, direction):
    route = []
    for n in range(lax.axis_size("sess")):
        y, x = n // SIDE, n % SIDE
        if direction < 2:
            x = (x + 1 - 2 * direction) % SIDE
        else:
            y = (y + 1 - 2 * (direction - 2)) % SIDE
        route.append((n, y * SIDE + x))
    return lax.ppermute(block, "sess", route)


def session_kernel(
    codes, pages, prefix, base, c, b, scaled, cumul, gate, carry, queries, new, state, pool, *refs
):
    received, (gated, squares, fresh, out, held, sem) = refs[:-6], refs[-6:]
    s = pl.program_id(0)
    slots = pl.num_programs(0)
    heads, width, depth = fresh.shape[1:]
    rows = state.shape[1]

    def fetch(at):
        item_copies(codes[at], pages, state, pool, received, held.at[at % 2], sem.at[at % 2])

    @pl.when(s == 0)
    def _():
        fetch(s)

    @pl.when(s + 1 < slots)
    def _():
        fetch(s + 1)

    now = held.at[s % 2]
    pltpu.make_async_copy(now, now, sem.at[s % 2]).wait()
    attend_step(now[rows:], queries[...], new[...], prefix[s], out)
    mamba_step(
        now[:rows].reshape(heads, width, depth),
        base[...], c[...], b[...], scaled[...], cumul[0], gate[...], carry[0],
        gated, squares, fresh,
    )


def sessions(
    codes, pages, prefix, base, c, b, scaled, cumul, gate, carry, queries, new, state, pool,
    received, shape,
):
    slots, tokens, heads = cumul.shape
    total, width = base.shape

    def own(block):
        rest = (0,) * (len(block) - 1)
        return pl.BlockSpec(block, lambda s: (s,) + rest)

    smem = pl.BlockSpec(memory_space=pltpu.SMEM)
    hbm = pl.BlockSpec(memory_space=pltpu.HBM)
    rows = state.shape[1] + pages.shape[0] // slots * pool.shape[1]
    return pl.pallas_call(
        session_kernel,
        grid=(slots,),
        in_specs=[
            smem,
            smem,
            smem,
            own((tokens, width)),
            own((tokens, NS)),
            own((tokens, NS)),
            own((tokens, width)),
            own((1, tokens, heads)),
            own((tokens, width)),
            own((1, heads, NS)),
            own((tokens, width)),
            own((tokens, new.shape[1])),
        ]
        + [hbm] * (2 + len(received)),
        out_specs=[
            own((tokens, width)),
            own((1, 1, tokens)),
            own((1,) + shape[1:]),
            own((tokens, width)),
        ],
        out_shape=[
            jax.ShapeDtypeStruct((total, width), F32),
            jax.ShapeDtypeStruct((slots, 1, tokens), F32),
            jax.ShapeDtypeStruct(shape, BF16),
            jax.ShapeDtypeStruct((total, width), BF16),
        ],
        scratch_shapes=[
            pltpu.VMEM((2, rows, state.shape[2]), BF16),
            pltpu.SemaphoreType.DMA((2,)),
        ],
        compiler_params=params(),
        cost_estimate=cost(2 * 10**9, 32 * 2**20),
        name="sessions",
    )(
        codes, pages, prefix, base, c, b, scaled, cumul, gate, carry, queries, new, state, pool,
        *received,
    )


def shards(
    mamba_x,
    gate_z,
    proj_bc,
    step_raw,
    step_bias,
    decay_log,
    skip_gain,
    norm_gain,
    state_cache,
    cache_slot,
    prefix_pages,
    page_table,
    queries,
    appended_memory_pair,
    key_value_pages,
):
    slots, heads = state_cache.shape[:2]
    count = cache_slot.shape[0]
    total = mamba_x.shape[0]
    tokens = total // slots
    me = lax.axis_index("sess")
    names = jnp.arange(count, dtype=jnp.int32)
    holds = (cache_slot[:, None] == names[None, :]).astype(jnp.int32)
    dest = jnp.sum(holds * (names // slots)[:, None], axis=0, keepdims=True)
    table, final = schedule(dest, count // slots)
    needed = jnp.max(jnp.where(final < slots, 0, (final - slots) // 4 + 1))
    done = jnp.max(final) < 127
    choice = jnp.sum((needed > jnp.array(STEPS, jnp.int32)).astype(jnp.int32))
    choice = jnp.where(done, choice, len(STEPS))
    sends = lax.dynamic_index_in_dim(table, me, 0, keepdims=False)
    local = jnp.arange(slots, dtype=jnp.int32)
    at_home = (cache_slot[:, None] == (me * slots + local)[None, :]).astype(jnp.int32)
    pages = jnp.sum(at_home[:, :, None] * page_table[:, None, :], axis=0).reshape(-1)
    mine = lax.dynamic_slice_in_dim(cache_slot, me * slots, slots)
    codes = jnp.sum((mine[:, None] == names[None, :]).astype(jnp.int32) * final, axis=1)

    def run(steps, _):
        pool = key_value_pages.reshape(key_value_pages.shape[:2] + (2 * HEAD_WIDTH,))
        state = state_cache.reshape(slots, heads * P_SIZE, NS)
        received = []
        for t in range(steps):
            ready = received[: 4 * max(0, t - DELAY)]
            sent = gather(t, sends, pages, state, pool, ready)
            received += [shift(block, d) for d, block in enumerate(sent)]

        group = lax.axis_index("mp") * heads // (HM // G)
        both = lax.dynamic_index_in_dim(proj_bc, group, axis=2, keepdims=False)
        b, c = both[:, 0], both[:, 1]
        delta = jax.nn.softplus(step_raw + step_bias[:, None]).reshape(heads, slots, tokens)
        falloff = -jnp.exp(decay_log)[:, None, None] * delta
        position = jnp.arange(tokens)
        lower = (position[:, None] >= position[None, :]).astype(F32)
        cumul = jnp.einsum("hsu,tu->hst", falloff, lower, precision=HIGHEST)
        last = cumul[:, :, tokens - 1 :]
        tail = (jnp.exp(last - cumul) * delta).transpose(1, 2, 0)
        carry = jnp.exp(last[:, :, 0]).T[:, :, None]
        carry = jnp.broadcast_to(carry, (slots, heads, NS))
        rows = jnp.stack([cumul, delta], axis=0).transpose(2, 0, 1, 3)
        rows = rows.reshape(slots, 2, heads * tokens)
        cumul = cumul.transpose(1, 2, 0)
        skip = jnp.repeat(skip_gain, P_SIZE)[None, :]
        base, scaled = mamba_before(mamba_x, b, c, cumul, tail, rows, skip)
        new = appended_memory_pair.reshape(total, 2 * HEAD_WIDTH)

        gated, squares, fresh, out = sessions(
            codes, pages, prefix_pages, base, c, b, scaled, cumul, gate_z, carry, queries, new,
            state, pool, received, state_cache.shape,
        )
        squares = squares.reshape(total)
        squares = squares + swapped(squares, "mp", 0)
        scale = lax.rsqrt(squares / (HM // G * P_SIZE) + EPS)
        mixed = (gated * scale[:, None] * norm_gain[None, :]).astype(BF16)
        return mixed, fresh, out

    def slow(_):
        return padded(
            mamba_x, gate_z, proj_bc, step_raw, step_bias, decay_log, skip_gain, norm_gain,
            state_cache, cache_slot, prefix_pages, page_table, queries, appended_memory_pair,
            key_value_pages,
        )

    return lax.switch(choice, [functools.partial(run, n) for n in STEPS] + [slow], 0)


def solution(mesh):
    return jax.shard_map(
        shards,
        mesh=mesh,
        in_specs=(
            P("sess", "mp"),
            P("sess", "mp"),
            P("sess", None, None, None),
            P("mp", "sess"),
            P("mp"),
            P("mp"),
            P("mp"),
            P("mp"),
            P("sess", "mp", None, None),
            P(),
            P("sess"),
            P(),
            P("sess", "mp"),
            P("sess", None, "mp", None),
            P("sess", None, None, "mp", None),
        ),
        out_specs=(P("sess", "mp"), P("sess", "mp", None, None), P("sess", "mp")),
        check_vma=False,
    )
```

```python
import functools

import jax
import jax.numpy as jnp
from jax import lax
from jax.experimental import pallas as pl
from jax.experimental.pallas import tpu as pltpu
from jax.sharding import PartitionSpec as P

HM = 128
P_SIZE = 64
NS = 256
G = 4
HEAD_WIDTH = 128
PAGE_TOKENS = 64
EPS = 1e-05

STEPS = (10, 14)
EARLY = 1
LOST = 127
DELAY = 1
SIDE = 4
HIGHEST = lax.Precision.HIGHEST
F32 = jnp.float32
BF16 = jnp.bfloat16


def params():
    return pltpu.CompilerParams(vmem_limit_bytes=56 * 1024 * 1024)


def cost(flops, moved):
    return pl.CostEstimate(flops=flops, bytes_accessed=moved, transcendentals=0)


def swapped(block, axis, stride):
    count = lax.axis_size(axis)
    route = []
    for low in range(count):
        high = low | 1 << stride
        if high != low and high < count:
            route += [(low, high), (high, low)]
    return lax.ppermute(block, axis, route)


def dot(a, b, dims, precision=None):
    return lax.dot_general(
        a, b, ((dims[:1], dims[1:]), ((), ())), precision=precision, preferred_element_type=F32
    )


def spread_matrix(heads, lanes):
    row = lax.broadcasted_iota(jnp.int32, (heads, heads * lanes), 0)
    column = lax.broadcasted_iota(jnp.int32, (heads, heads * lanes), 1)
    return (row == column // lanes).astype(BF16)


def spread(columns, lanes):
    parts = []
    for _ in range(3):
        parts.append(columns.astype(BF16))
        columns = columns - parts[-1].astype(F32)
    matrix = spread_matrix(columns.shape[1], lanes)
    return dot(jnp.concatenate(parts, axis=1), jnp.concatenate([matrix] * 3, axis=0), (1, 0))


def before_kernel(x_ref, b_ref, c_ref, cumul_ref, tail_ref, row_ref, skip_ref, base, scaled):
    heads = cumul_ref.shape[2]
    tokens = x_ref.shape[0]
    quad = 4
    x = x_ref[...]
    inner = dot(c_ref[...], b_ref[...], (1, 1))
    at_t = spread(cumul_ref[0], tokens)
    row = lax.broadcasted_iota(jnp.int32, at_t.shape, 0)
    column = lax.broadcasted_iota(jnp.int32, at_t.shape, 1)
    causal = row >= column % tokens
    gap = at_t - row_ref[0, 0:1]
    decay = jnp.where(causal, jnp.exp(jnp.where(causal, gap, 0.0)), 0.0)
    inner = jnp.concatenate([inner] * heads, axis=1)
    weights = (inner * decay * row_ref[0, 1:2]).astype(BF16)
    own_row = lax.broadcasted_iota(jnp.int32, (quad * tokens, quad * P_SIZE), 0) // tokens
    own_column = lax.broadcasted_iota(jnp.int32, (quad * tokens, quad * P_SIZE), 1) // P_SIZE
    own = own_row == own_column
    for q in range(heads // quad):
        lanes = slice(q * quad * P_SIZE, (q + 1) * quad * P_SIZE)
        values = x[:, lanes].astype(F32)
        stacked = jnp.where(own, jnp.concatenate([values] * quad, axis=0), 0.0).astype(BF16)
        part = weights[:, q * quad * tokens : (q + 1) * quad * tokens]
        base[:, lanes] = dot(part, stacked, (1, 0)) + skip_ref[:, lanes] * values
    scaled[...] = (x.astype(F32) * spread(tail_ref[0], P_SIZE)).astype(BF16)


def mamba_before(x, b, c, cumul, tail, rows, skip):
    total, width = x.shape
    slots, tokens, heads = cumul.shape
    per = lambda shape: pl.BlockSpec(shape, lambda s: (s,) + (0,) * (len(shape) - 1))
    return pl.pallas_call(
        before_kernel,
        grid=(slots,),
        in_specs=[
            per((tokens, width)),
            per((tokens, NS)),
            per((tokens, NS)),
            per((1, tokens, heads)),
            per((1, tokens, heads)),
            per((1, 2, heads * tokens)),
            pl.BlockSpec((1, width), lambda s: (0, 0)),
        ],
        out_specs=[per((tokens, width)), per((tokens, width))],
        out_shape=[
            jax.ShapeDtypeStruct((total, width), F32),
            jax.ShapeDtypeStruct((total, width), BF16),
        ],
        compiler_params=params(),
        cost_estimate=cost(10**9, 20 * 2**20),
        name="mamba_before",
    )(x, b, c, cumul, tail, rows, skip)


def mamba_step(state, base, c, b, scaled, cumul, gate, carry, gated, squares, fresh):
    heads = state.shape[0]
    carried = dot(c, state.reshape(heads * P_SIZE, NS), (1, 1))
    out = base + carried * spread(jnp.exp(cumul), P_SIZE)
    gate = gate.astype(F32)
    value = out * (gate / (1.0 + jnp.exp(-gate)))
    gated[...] = value
    ones = jnp.ones((8, value.shape[1]), F32)
    squares[0] = dot(ones, value * value, (1, 1), HIGHEST)[0:1]
    local = dot(scaled, b, (0, 0))
    for h in range(heads):
        rows = slice(h * P_SIZE, (h + 1) * P_SIZE)
        fresh[0, h] = (carry[h : h + 1] * state[h].astype(F32) + local[rows]).astype(BF16)


def attend_step(pages, queries, new, prefix, out):
    kept = pages.shape[0]
    tokens = queries.shape[0]
    heads = queries.shape[1] // HEAD_WIDTH
    q = jnp.concatenate(
        [queries[:, g * HEAD_WIDTH : (g + 1) * HEAD_WIDTH] for g in range(heads)], axis=0
    )
    factor = HEAD_WIDTH ** (-0.5)
    old_scores = dot(q, pages[:, :HEAD_WIDTH], (1, 1)) * factor
    new_scores = dot(q, new[:, :HEAD_WIDTH], (1, 1)) * factor
    column = lax.broadcasted_iota(jnp.int32, old_scores.shape, 1)
    old_scores = jnp.where(column < prefix * PAGE_TOKENS, old_scores, -jnp.inf)
    row = lax.broadcasted_iota(jnp.int32, new_scores.shape, 0) % tokens
    column = lax.broadcasted_iota(jnp.int32, new_scores.shape, 1)
    new_scores = jnp.where(column <= row, new_scores, -jnp.inf)
    peak = jnp.maximum(
        jnp.max(old_scores, axis=1, keepdims=True), jnp.max(new_scores, axis=1, keepdims=True)
    )
    old_expo = jnp.exp(old_scores - peak)
    new_expo = jnp.exp(new_scores - peak)
    total = jnp.sum(old_expo, axis=1, keepdims=True) + jnp.sum(new_expo, axis=1, keepdims=True)
    old_probs = (old_expo / total).astype(BF16)
    new_probs = (new_expo / total).astype(BF16)
    mixed = dot(old_probs, pages[:, HEAD_WIDTH:], (1, 0)) + dot(
        new_probs, new[:, HEAD_WIDTH:], (1, 0)
    )
    for g in range(heads):
        out[:, g * HEAD_WIDTH : (g + 1) * HEAD_WIDTH] = mixed[
            g * tokens : (g + 1) * tokens
        ].astype(BF16)


def schedule_kernel(first, last, dest_ref, *refs):
    old_table, old_items, table_ref, items_ref = refs if len(refs) == 4 else (None, None) + refs
    dest = dest_ref[...]
    items = dest.shape[1]
    nodes = table_ref.shape[0]
    lane = lax.broadcasted_iota(jnp.int32, (1, items), 1)
    node = lax.broadcasted_iota(jnp.int32, (nodes, items), 0)
    slot = lax.broadcasted_iota(jnp.int32, table_ref.shape, 1)
    per = items // nodes
    yd, xd = dest // SIDE, dest % SIDE

    def step(t, carry):
        y, x, code, ready, table = carry
        ry, rx = (yd - y) & (SIDE - 1), (xd - x) & (SIDE - 1)
        want = [
            (rx == 1) | (rx == 2),
            (rx == 3) | (rx == 2),
            (ry == 1) | (ry == 2),
            (ry == 3) | (ry == 2),
        ]
        want = [w.astype(F32) for w in want]
        ways = want[0] + want[1] + want[2] + want[3]
        share = jnp.where(ways > 0.0, 12.0 / jnp.maximum(ways, 1.0), 0.0)
        left = (jnp.minimum(rx, SIDE - rx) + jnp.minimum(ry, SIDE - ry)).astype(F32)
        here = ((node == y * SIDE + x) & (ready <= t)).astype(F32)
        demand = [jnp.sum(here * (w * share), axis=1, keepdims=True) for w in want]
        pull = sum(w * d for w, d in zip(want, demand))
        rank = []
        for a in range(4):
            lower = 0.0
            for b in range(4):
                if b != a:
                    under = demand[b] <= demand[a] if b < a else demand[b] < demand[a]
                    lower = lower + under.astype(F32)
            rank.append(lower)
        free = here
        code_f = code.astype(F32)
        moves = [jnp.zeros((nodes, items), F32) for _ in range(4)]
        for r in range(4):
            turn = [(k == float(r)).astype(F32) for k in rank]
            wanted = sum(w * u for w, u in zip(want, turn)) * free
            own = sum(d * u for d, u in zip(demand, turn))
            value = left * 192.0 + (pull - own)
            key = jnp.where(wanted > 0.0, jnp.floor(value + 0.5) * 128.0 + (127.0 - code_f), -1.0)
            best = jnp.max(key, axis=1, keepdims=True)
            taken = ((key == best) & (best >= 0.0)).astype(F32)
            free = free * (1.0 - taken)
            picked = 127 - (best.astype(jnp.int32) & 127)
            for d in range(4):
                moves[d] = moves[d] + taken * turn[d]
                here_now = (slot == t * 4 + d) & (turn[d] > 0.0) & (best >= 0.0)
                table = jnp.where(here_now, picked, table)
        gone = [jnp.sum(m, axis=0, keepdims=True).astype(jnp.int32) for m in moves]
        x = (x + gone[0] - gone[1]) & (SIDE - 1)
        y = (y + gone[2] - gone[3]) & (SIDE - 1)
        for d in range(4):
            code = jnp.where(gone[d] > 0, per + t * 4 + d, code)
        ready = jnp.where(gone[0] + gone[1] + gone[2] + gone[3] > 0, t + 1 + DELAY, ready)
        return y, x, code, ready, table

    if old_table is None:
        at = lane // per
        state = (at // SIDE, at % SIDE, lane % per, jnp.zeros((1, items), jnp.int32))
        table = jnp.full(table_ref.shape, -1, jnp.int32)
    else:
        state = tuple(old_items[n : n + 1] for n in range(4))
        table = old_table[...]
    y, x, code, ready, table = lax.fori_loop(first, last, step, state + (table,))
    table_ref[...] = table
    for n, row in enumerate((y, x, code, ready)):
        items_ref[n : n + 1] = row
    items_ref[4:5] = y * SIDE + x
    items_ref[5:6] = jnp.where(y * SIDE + x == dest, code, LOST)
    items_ref[6:8] = jnp.zeros((2, items), jnp.int32)


def schedule(dest, nodes, first, last, before=()):
    return pl.pallas_call(
        functools.partial(schedule_kernel, first, last),
        out_shape=[
            jax.ShapeDtypeStruct((nodes, 128), jnp.int32),
            jax.ShapeDtypeStruct((8, dest.shape[1]), jnp.int32),
        ],
        compiler_params=params(),
        cost_estimate=cost(10**7, 2**20),
        name="schedule",
    )(dest, *before)


def item_copies(code, pages, state, pool, target, sem):
    local = state.shape[0]
    rows = state.shape[1]
    per = pages.shape[0] // local
    tokens = pool.shape[1]

    @pl.when((code >= 0) & (code < local))
    def _():
        pltpu.make_async_copy(state.at[code], target.at[pl.ds(0, rows)], sem).start()
        for m in range(per):
            pltpu.make_async_copy(
                pool.at[pages[code * per + m]],
                target.at[pl.ds(rows + m * tokens, tokens)],
                sem,
            ).start()


def gather_kernel(t, codes, pages, state, pool, previous, *refs):
    received, targets, (held, sem, out_sem) = refs[:-7], refs[-7:-3], refs[-3:]
    local = state.shape[0]
    wanted = [codes[4 * t + d] for d in range(4)]

    def load(d, carry):
        item_copies(codes[4 * t + d], pages, state, pool, held.at[d], sem.at[d])
        return carry

    lax.fori_loop(0, 4, load, 0)
    for b, source in enumerate(received):
        hits = [(code == local + b).astype(jnp.int32) for code in wanted]

        @pl.when(hits[0] + hits[1] + hits[2] + hits[3] > 0)
        def _(source=source, d=hits[1] + 2 * hits[2] + 3 * hits[3]):
            pltpu.make_async_copy(source, held.at[d], sem.at[d]).start()

    def store(d):
        return pltpu.make_async_copy(held.at[d], targets[d], out_sem.at[d])

    for d in range(4):

        @pl.when(wanted[d] >= 0)
        def _(d=d):
            pltpu.make_async_copy(held.at[d], held.at[d], sem.at[d]).wait()
            store(d).start()

    for d in range(4):

        @pl.when(wanted[d] >= 0)
        def _(d=d):
            store(d).wait()


def gather(t, codes, pages, state, pool, previous, received):
    rows = state.shape[1] + pages.shape[0] // state.shape[0] * pool.shape[1]
    smem = pl.BlockSpec(memory_space=pltpu.SMEM)
    anywhere = pl.BlockSpec(memory_space=pl.ANY)
    out = jax.ShapeDtypeStruct((rows, state.shape[2]), state.dtype)
    return pl.pallas_call(
        functools.partial(gather_kernel, t),
        in_specs=[smem, smem] + [anywhere] * (3 + len(received)),
        out_specs=[pl.BlockSpec(memory_space=pltpu.HBM)] * 4,
        out_shape=[out] * 4,
        scratch_shapes=[
            pltpu.VMEM((4, rows, state.shape[2]), state.dtype),
            pltpu.SemaphoreType.DMA((4,)),
            pltpu.SemaphoreType.DMA((4,)),
        ],
        compiler_params=params(),
        cost_estimate=cost(0, 16 * rows * state.shape[2]),
        name="gather_step",
    )(codes, pages, state, pool, previous, *received)


def blank_kernel(*refs):
    pass


def blank(shapes):
    hbm = pl.BlockSpec(memory_space=pltpu.HBM)
    return pl.pallas_call(
        blank_kernel,
        out_specs=[hbm] * len(shapes),
        out_shape=shapes,
        compiler_params=params(),
        name="blank",
    )()


def shift(block, direction):
    route = []
    for n in range(lax.axis_size("sess")):
        y, x = n // SIDE, n % SIDE
        if direction < 2:
            x = (x + 1 - 2 * direction) % SIDE
        else:
            y = (y + 1 - 2 * (direction - 2)) % SIDE
        route.append((n, y * SIDE + x))
    return lax.ppermute(block, "sess", route)


def session_kernel(
    codes, pages, prefix, base, c, b, scaled, cumul, gate, carry, queries, new, state, pool, *refs
):
    received, late, (gated, squares, fresh, out, held, sem) = refs[:-7], refs[-7], refs[-6:]
    at = pl.program_id(0)
    slots = pl.num_programs(0) - 1
    heads, width, depth = fresh.shape[1:]
    rows = state.shape[1]

    @pl.when(at < slots)
    def _():
        code = codes[at]
        target, done = held.at[at % 2], sem.at[at % 2]
        item_copies(code, pages, state, pool, target, done)
        for b, source in enumerate(received):

            @pl.when(code == state.shape[0] + b)
            def _(source=source):
                pltpu.make_async_copy(source, target, done).start()

        @pl.when(code == LOST)
        def _():
            pltpu.make_async_copy(late.at[at], target, done).start()

    @pl.when(at > 0)
    def _():
        s = at - 1
        now = held.at[s % 2]
        pltpu.make_async_copy(now, now, sem.at[s % 2]).wait()
        attend_step(now[rows:], queries[...], new[...], prefix[s], out)
        mamba_step(
            now[:rows].reshape(heads, width, depth),
            base[...], c[...], b[...], scaled[...], cumul[0], gate[...], carry[0],
            gated, squares, fresh,
        )


def sessions(
    codes, pages, prefix, base, c, b, scaled, cumul, gate, carry, queries, new, state, pool,
    received, late, shape,
):
    slots, tokens, heads = cumul.shape
    total, width = base.shape

    def own(block):
        rest = (0,) * (len(block) - 1)
        return pl.BlockSpec(block, lambda s: (jnp.maximum(s - 1, 0),) + rest)

    smem = pl.BlockSpec(memory_space=pltpu.SMEM)
    anywhere = pl.BlockSpec(memory_space=pl.ANY)
    return pl.pallas_call(
        session_kernel,
        grid=(slots + 1,),
        in_specs=[
            smem,
            smem,
            smem,
            own((tokens, width)),
            own((tokens, NS)),
            own((tokens, NS)),
            own((tokens, width)),
            own((1, tokens, heads)),
            own((tokens, width)),
            own((1, heads, NS)),
            own((tokens, width)),
            own((tokens, new.shape[1])),
        ]
        + [anywhere] * (3 + len(received)),
        out_specs=[
            own((tokens, width)),
            own((1, 1, tokens)),
            own((1,) + shape[1:]),
            own((tokens, width)),
        ],
        out_shape=[
            jax.ShapeDtypeStruct((total, width), F32),
            jax.ShapeDtypeStruct((slots, 1, tokens), F32),
            jax.ShapeDtypeStruct(shape, BF16),
            jax.ShapeDtypeStruct((total, width), BF16),
        ],
        scratch_shapes=[
            pltpu.VMEM((2,) + late.shape[1:], BF16),
            pltpu.SemaphoreType.DMA((2,)),
        ],
        compiler_params=params(),
        cost_estimate=cost(2 * 10**9, 32 * 2**20),
        name="sessions",
    )(
        codes, pages, prefix, base, c, b, scaled, cumul, gate, carry, queries, new, state, pool,
        *received, late,
    )


def shards(
    mamba_x,
    gate_z,
    proj_bc,
    step_raw,
    step_bias,
    decay_log,
    skip_gain,
    norm_gain,
    state_cache,
    cache_slot,
    prefix_pages,
    page_table,
    queries,
    appended_memory_pair,
    key_value_pages,
):
    slots, heads = state_cache.shape[:2]
    count = cache_slot.shape[0]
    total = mamba_x.shape[0]
    tokens = total // slots
    me = lax.axis_index("sess")
    nodes = count // slots
    names = jnp.arange(count, dtype=jnp.int32)
    holds = (cache_slot[:, None] == names[None, :]).astype(jnp.int32)
    session = jnp.sum(holds * names[:, None], axis=0, keepdims=True)
    dest = session // slots

    def row(table):
        return lax.dynamic_index_in_dim(table, me, 0, keepdims=False)

    early = schedule(dest, nodes, 0, EARLY)
    table, items = schedule(dest, nodes, EARLY, STEPS[1], early)
    early_sends, sends = row(early[0]), row(table)
    final = items[5]
    needed = jnp.max(jnp.where(items[2] < slots, 0, (items[2] - slots) // 4 + 1))
    local = jnp.arange(slots, dtype=jnp.int32)
    at_home = (cache_slot[:, None] == (me * slots + local)[None, :]).astype(jnp.int32)
    pages = jnp.sum(at_home[:, :, None] * page_table[:, None, :], axis=0).reshape(-1)
    mine = lax.dynamic_slice_in_dim(cache_slot, me * slots, slots)
    codes = jnp.sum((mine[:, None] == names[None, :]).astype(jnp.int32) * final, axis=1)

    pool = key_value_pages.reshape(key_value_pages.shape[:2] + (2 * HEAD_WIDTH,))
    state = state_cache.reshape(slots, heads * P_SIZE, NS)
    item = (heads * P_SIZE + page_table.shape[1] * PAGE_TOKENS, NS)

    def step(t, sent, received):
        ready = received[: 4 * max(0, t - DELAY)]
        plan = early_sends if t < EARLY else sends
        sent = gather(t, plan, pages, state, pool, sent[0], ready)
        return sent, received + [shift(block, d) for d, block in enumerate(sent)]

    sent, received = [pool], []
    for t in range(STEPS[0]):
        sent, received = step(t, sent, received)

    def deliver(received, held):
        def body(carry):
            left, held = carry
            c = jnp.argmax(left)
            code = items[2][c]
            block = gather(0, jnp.stack([code, -1, -1, -1]), pages, state, pool, pool, received)[0]
            to = session[0][c]
            place = to % slots
            old = lax.dynamic_index_in_dim(held, place, 0, keepdims=False)
            ring = [(n, (n + 1) % nodes) for n in range(nodes)]

            def turn(r, carry):
                block, kept = carry
                block = lax.ppermute(block, "sess", ring)
                mine = (to // slots == me) & ((items[4][c] + r) % nodes == me)
                return block, jnp.where(mine, block, kept)

            block = lax.fori_loop(1, nodes, turn, (block, old))[1]
            held = lax.dynamic_update_index_in_dim(held, block, place, 0)
            return left.at[c].set(0), held

        left = (final == LOST).astype(jnp.int32)
        return lax.while_loop(lambda carry: jnp.max(carry[0]) > 0, body, (left, held))[1]

    def shapes(t):
        kinds = [jax.ShapeDtypeStruct(item, BF16)] * (4 * (STEPS[1] - t))
        return kinds + [jax.ShapeDtypeStruct((slots,) + item, BF16)]

    def late_steps(t, received):
        if t == STEPS[1]:
            return [deliver(received, blank(shapes(t))[0])]

        def more(_):
            after = step(t, [pool], received)[1]
            return after[4 * t :] + late_steps(t + 1, after)

        return list(lax.cond(needed > t, more, lambda _: list(blank(shapes(t))), 0))

    rest = late_steps(STEPS[0], received)
    received, late = received + rest[:-1], rest[-1]

    group = lax.axis_index("mp") * heads // (HM // G)
    both = lax.dynamic_index_in_dim(proj_bc, group, axis=2, keepdims=False)
    b, c = both[:, 0], both[:, 1]
    delta = jax.nn.softplus(step_raw + step_bias[:, None]).reshape(heads, slots, tokens)
    falloff = -jnp.exp(decay_log)[:, None, None] * delta
    position = jnp.arange(tokens)
    lower = (position[:, None] >= position[None, :]).astype(F32)
    cumul = jnp.einsum("hsu,tu->hst", falloff, lower, precision=HIGHEST)
    last = cumul[:, :, tokens - 1 :]
    tail = (jnp.exp(last - cumul) * delta).transpose(1, 2, 0)
    carry = jnp.exp(last[:, :, 0]).T[:, :, None]
    carry = jnp.broadcast_to(carry, (slots, heads, NS))
    rows = jnp.stack([cumul, delta], axis=0).transpose(2, 0, 1, 3)
    rows = rows.reshape(slots, 2, heads * tokens)
    cumul = cumul.transpose(1, 2, 0)
    skip = jnp.repeat(skip_gain, P_SIZE)[None, :]
    base, scaled = mamba_before(mamba_x, b, c, cumul, tail, rows, skip)
    new = appended_memory_pair.reshape(total, 2 * HEAD_WIDTH)

    gated, squares, fresh, out = sessions(
        codes, pages, prefix_pages, base, c, b, scaled, cumul, gate_z, carry, queries, new,
        state, pool, received, late, state_cache.shape,
    )
    squares = squares.reshape(total)
    squares = squares + swapped(squares, "mp", 0)
    scale = lax.rsqrt(squares / (HM // G * P_SIZE) + EPS)
    mixed = (gated * scale[:, None] * norm_gain[None, :]).astype(BF16)
    return mixed, fresh, out


def solution(mesh):
    return jax.shard_map(
        shards,
        mesh=mesh,
        in_specs=(
            P("sess", "mp"),
            P("sess", "mp"),
            P("sess", None, None, None),
            P("mp", "sess"),
            P("mp"),
            P("mp"),
            P("mp"),
            P("mp"),
            P("sess", "mp", None, None),
            P(),
            P("sess"),
            P(),
            P("sess", "mp"),
            P("sess", None, "mp", None),
            P("sess", None, None, "mp", None),
        ),
        out_specs=(P("sess", "mp"), P("sess", "mp", None, None), P("sess", "mp")),
        check_vma=False,
    )
```

```python
import functools

import jax
import jax.numpy as jnp
from jax import lax
from jax.experimental import pallas as pl
from jax.experimental.pallas import tpu as pltpu
from jax.sharding import PartitionSpec as P

HM = 128
P_SIZE = 64
NS = 256
G = 4
HEAD_WIDTH = 128
PAGE_TOKENS = 64
EPS = 1e-05

STEPS = (10, 12)
PARTS = (1, 3, 6, 9, 12)
FROM = 6
TOGETHER = 2
LOST = 127
DELAY = 1
SIDE = 4
HIGHEST = lax.Precision.HIGHEST
F32 = jnp.float32
BF16 = jnp.bfloat16


def params():
    return pltpu.CompilerParams(vmem_limit_bytes=56 * 1024 * 1024)


def cost(flops, moved):
    return pl.CostEstimate(flops=flops, bytes_accessed=moved, transcendentals=0)


def swapped(block, axis, stride):
    count = lax.axis_size(axis)
    route = []
    for low in range(count):
        high = low | 1 << stride
        if high != low and high < count:
            route += [(low, high), (high, low)]
    return lax.ppermute(block, axis, route)


def dot(a, b, dims, precision=None):
    return lax.dot_general(
        a, b, ((dims[:1], dims[1:]), ((), ())), precision=precision, preferred_element_type=F32
    )


def spread(columns, matrix):
    parts = []
    for _ in range(3):
        parts.append(columns.astype(BF16))
        columns = columns - parts[-1].astype(F32)
    return dot(jnp.concatenate(parts, axis=1), matrix, (1, 0))


def spread_matrix(heads, lanes):
    return jnp.tile(jnp.repeat(jnp.eye(heads, dtype=BF16), lanes, axis=1), (3, 1))


def prepare_kernel(raw_ref, bias_ref, log_ref, ct_ref, cd_ref):
    heads, total = raw_ref.shape
    slots, tokens = ct_ref.shape[:2]
    wide = 128
    each = wide // tokens
    eye = lax.broadcasted_iota(jnp.int32, (heads, heads), 0) == lax.broadcasted_iota(
        jnp.int32, (heads, heads), 1
    )

    def column(ref):
        return jnp.sum(jnp.where(eye, ref[...], 0.0), axis=1, keepdims=True)

    source = lax.broadcasted_iota(jnp.int32, (wide, wide), 0)
    target = lax.broadcasted_iota(jnp.int32, (wide, wide), 1)
    own = source // tokens == target // tokens
    until = (own & (source <= target)).astype(F32)
    final = (own & (source % tokens == tokens - 1)).astype(F32)
    bias, rate = column(bias_ref), -jnp.exp(column(log_ref))
    for n in range(total // wide):
        raw = raw_ref[:, n * wide : (n + 1) * wide] + bias
        delta = jnp.maximum(raw, 0.0) + jnp.log1p(jnp.exp(-jnp.abs(raw)))
        cumul = dot(rate * delta, until, (1, 0), HIGHEST)
        tail = jnp.exp(dot(cumul, final, (1, 0), HIGHEST) - cumul) * delta
        turned = jnp.concatenate([cumul, tail], axis=0).T
        both = jnp.concatenate([cumul, delta], axis=0)
        for k in range(each):
            ct_ref[n * each + k] = turned[k * tokens : (k + 1) * tokens]
            cd_ref[n * each + k] = both[:, k * tokens : (k + 1) * tokens]


def prepare(step_raw, step_bias, decay_log, slots):
    heads, total = step_raw.shape
    tokens = total // slots
    return pl.pallas_call(
        prepare_kernel,
        out_shape=[
            jax.ShapeDtypeStruct((slots, tokens, 2 * heads), F32),
            jax.ShapeDtypeStruct((slots, 2 * heads, tokens), F32),
        ],
        compiler_params=params(),
        cost_estimate=cost(10**7, 2**20),
        name="prepare",
    )(step_raw, step_bias[None, :], decay_log[None, :])


def mamba_step(state, x, bc, ct, cd, skip, spread32, spread64, own, gate, gated, squares, fresh):
    heads, width, _ = state.shape
    tokens = x.shape[0]
    quad = own.shape[1] // width
    b, c = bc[:, :NS], bc[:, NS:]
    cumul = ct[:, :heads]
    flat = [
        jnp.concatenate([cd[n * heads + h : n * heads + h + 1] for h in range(heads)], axis=1)
        for n in range(2)
    ]
    carry = jnp.exp(cd[:heads, tokens - 1 :])
    inner = dot(c, b, (1, 1))
    at_t = spread(cumul, spread32)
    place = lax.broadcasted_iota(jnp.int32, at_t.shape, 0)
    column = lax.broadcasted_iota(jnp.int32, at_t.shape, 1)
    causal = place >= column % tokens
    decay = jnp.exp(jnp.where(causal, at_t - flat[0], -jnp.inf))
    inner = jnp.concatenate([inner] * heads, axis=1)
    weights = (inner * decay * flat[1]).astype(BF16)
    base = []
    for q in range(heads // quad):
        part = x[:, q * quad * width : (q + 1) * quad * width]
        stacked = jnp.concatenate([part] * quad, axis=0) * own
        base.append(dot(weights[:, q * quad * tokens : (q + 1) * quad * tokens], stacked, (1, 0)))
    values = x.astype(F32)
    scaled = (values * spread(ct[:, heads:], spread64)).astype(BF16)
    carried = dot(c, state.reshape(heads * width, NS), (1, 1))
    out = (
        jnp.concatenate(base, axis=1)
        + carried * spread(jnp.exp(cumul), spread64)
        + spread(skip, spread64) * values
    )
    gate = gate.astype(F32)
    value = out * (gate / (1.0 + jnp.exp(-gate)))
    gated[...] = value
    total = jnp.sum(value * value, axis=1, keepdims=True)
    squares[...] = jnp.broadcast_to(total, squares.shape)
    local = dot(scaled, b, (0, 0))
    for h in range(heads):
        rows = slice(h * width, (h + 1) * width)
        fresh[h] = (carry[h : h + 1] * state[h].astype(F32) + local[rows]).astype(BF16)


def attend_step(pages, queries, new, prefix, out):
    kept = pages.shape[0]
    tokens = queries.shape[0]
    heads = queries.shape[1] // HEAD_WIDTH
    q = jnp.concatenate(
        [queries[:, g * HEAD_WIDTH : (g + 1) * HEAD_WIDTH] for g in range(heads)], axis=0
    )
    factor = HEAD_WIDTH ** (-0.5)
    old_scores = dot(q, pages[:, :HEAD_WIDTH], (1, 1)) * factor
    new_scores = dot(q, new[:, :HEAD_WIDTH], (1, 1)) * factor
    column = lax.broadcasted_iota(jnp.int32, old_scores.shape, 1)
    old_scores = jnp.where(column < prefix * PAGE_TOKENS, old_scores, -jnp.inf)
    row = lax.broadcasted_iota(jnp.int32, new_scores.shape, 0) % tokens
    column = lax.broadcasted_iota(jnp.int32, new_scores.shape, 1)
    new_scores = jnp.where(column <= row, new_scores, -jnp.inf)
    peak = jnp.maximum(
        jnp.max(old_scores, axis=1, keepdims=True), jnp.max(new_scores, axis=1, keepdims=True)
    )
    old_expo = jnp.exp(old_scores - peak)
    new_expo = jnp.exp(new_scores - peak)
    total = jnp.sum(old_expo, axis=1, keepdims=True) + jnp.sum(new_expo, axis=1, keepdims=True)
    part = 1.0 / total
    old_probs = (old_expo * part).astype(BF16)
    new_probs = (new_expo * part).astype(BF16)
    mixed = dot(old_probs, pages[:, HEAD_WIDTH:], (1, 0)) + dot(
        new_probs, new[:, HEAD_WIDTH:], (1, 0)
    )
    for g in range(heads):
        out[:, g * HEAD_WIDTH : (g + 1) * HEAD_WIDTH] = mixed[
            g * tokens : (g + 1) * tokens
        ].astype(BF16)


def wanted_ways(ry, rx):
    return [
        (rx == 1) | (rx == 2),
        (rx == 3) | (rx == 2),
        (ry == 1) | (ry == 2),
        (ry == 3) | (ry == 2),
    ]


def schedule_kernel(first, last, slots, me, session_ref, *refs):
    table_ref, items_ref, plan_ref, info_ref = refs[-4:]
    old_table, old_items = refs[:-4] if len(refs) == 6 else (None, None)
    session = session_ref[...]
    dest = session // slots
    items = dest.shape[1]
    nodes = table_ref.shape[0]
    lane = lax.broadcasted_iota(jnp.int32, (1, items), 1)
    node = lax.broadcasted_iota(jnp.int32, (nodes, items), 0)
    slot = lax.broadcasted_iota(jnp.int32, table_ref.shape, 1)
    per = items // nodes
    yd, xd = dest // SIDE, dest % SIDE

    def step(t, carry):
        y, x, code, ready, table = carry
        ry, rx = (yd - y) & (SIDE - 1), (xd - x) & (SIDE - 1)
        want = [w.astype(F32) for w in wanted_ways(ry, rx)]
        ways = want[0] + want[1] + want[2] + want[3]
        share = jnp.where(ways > 0.0, 12.0 / jnp.maximum(ways, 1.0), 0.0)
        left = (jnp.minimum(rx, SIDE - rx) + jnp.minimum(ry, SIDE - ry)).astype(F32)
        at = y * SIDE + x
        weights = [w * share for w in want]

        def demands(place):
            here = place == at
            return [jnp.sum(jnp.where(here, w, 0.0), axis=1, keepdims=True) for w in weights]

        demand = demands(node)
        here = ((node == at) & (ready <= t)).astype(F32)
        ahead = []
        for d in range(4):
            ny, nx = node // SIDE, node % SIDE
            if d < 2:
                nx = (nx + 1 - 2 * d) & (SIDE - 1)
                left_x, left_y = (rx - 1 + 2 * d) & (SIDE - 1), ry
            else:
                ny = (ny + 1 - 2 * (d - 2)) & (SIDE - 1)
                left_x, left_y = rx, (ry - 1 + 2 * (d - 2)) & (SIDE - 1)
            there = demands(ny * SIDE + nx)
            least = jnp.full((nodes, items), 1e6, F32)
            for w, load in zip(wanted_ways(left_y, left_x), there):
                least = jnp.minimum(least, jnp.where(w, load, 1e6))
            ahead.append(jnp.where(least >= 1e6, 0.0, least))
        pull = sum(w * d for w, d in zip(want, demand))
        rank = []
        for a in range(4):
            lower = 0.0
            for b in range(4):
                if b != a:
                    under = demand[b] <= demand[a] if b < a else demand[b] < demand[a]
                    lower = lower + under.astype(F32)
            rank.append(lower)
        free = here
        code_f = code.astype(F32)
        moves = [jnp.zeros((nodes, items), F32) for _ in range(4)]
        for r in range(4):
            turn = [(k == float(r)).astype(F32) for k in rank]
            wanted = sum(w * u for w, u in zip(want, turn)) * free
            own = sum(d * u for d, u in zip(demand, turn))
            value = 4096.0 + left * 192.0 + (pull - own) - sum(a * u for a, u in zip(ahead, turn))
            value = jnp.maximum(value, 0.0)
            key = jnp.where(wanted > 0.0, jnp.floor(value + 0.5) * 128.0 + (127.0 - code_f), -1.0)
            best = jnp.max(key, axis=1, keepdims=True)
            taken = ((key == best) & (best >= 0.0)).astype(F32)
            free = free * (1.0 - taken)
            picked = 127 - (best.astype(jnp.int32) & 127)
            for d in range(4):
                moves[d] = moves[d] + taken * turn[d]
                here_now = (slot == t * 4 + d) & (turn[d] > 0.0) & (best >= 0.0)
                table = jnp.where(here_now, picked, table)
        gone = [jnp.sum(m, axis=0, keepdims=True).astype(jnp.int32) for m in moves]
        x = (x + gone[0] - gone[1]) & (SIDE - 1)
        y = (y + gone[2] - gone[3]) & (SIDE - 1)
        for d in range(4):
            code = jnp.where(gone[d] > 0, per + t * 4 + d, code)
        ready = jnp.where(gone[0] + gone[1] + gone[2] + gone[3] > 0, t + 1 + DELAY, ready)
        return y, x, code, ready, table

    if old_table is None:
        at = lane // per
        state = (at // SIDE, at % SIDE, lane % per, jnp.zeros((1, items), jnp.int32))
        table = jnp.full(table_ref.shape, -1, jnp.int32)
    else:
        state = tuple(old_items[n : n + 1] for n in range(4))
        table = old_table[...]
    y, x, code, ready, table = lax.fori_loop(first, last, step, state + (table,))
    table_ref[...] = table
    for n, row in enumerate((y, x, code, ready)):
        items_ref[n : n + 1] = row
    items_ref[4:5] = y * SIDE + x
    items_ref[5:6] = jnp.where(y * SIDE + x == dest, code, LOST)
    items_ref[6:8] = jnp.zeros((2, items), jnp.int32)
    row = lax.broadcasted_iota(jnp.int32, table.shape, 0)
    plan_ref[...] = jnp.sum(jnp.where(row == me[0], table, 0), axis=0, keepdims=True)
    if last == PARTS[-1]:
        final = jnp.where(y * SIDE + x == dest, code, LOST)
        came = jnp.where(final < per, 0, (final - per) // 4 + 1)
        key = jnp.where(dest == me[0], came * items + lane, -1)
        mine = jnp.sum(jnp.where(node == session - me[0] * slots, key, 0), axis=1, keepdims=True)
        rank = jnp.sum(((mine > key) & (key >= 0)).astype(F32), axis=1, keepdims=True)
        place = lax.broadcasted_iota(jnp.int32, (nodes, slots), 0)
        other = lax.broadcasted_iota(jnp.int32, (nodes, slots), 1)
        hot = (rank == other.astype(F32)).astype(F32)
        order = jnp.sum(hot * place.astype(F32), axis=0, keepdims=True)
        order = jnp.sum(jnp.where(place == other, order, 0.0), axis=1, keepdims=True)
        codes = jnp.sum(
            jnp.where(node == session - me[0] * slots, final, 0), axis=1, keepdims=True
        )
        ready = ((key >= 0) & (came + DELAY <= node)).astype(F32)
        here = jnp.minimum(jnp.sum(ready, axis=1, keepdims=True), slots - 1.0)
        info = jnp.where(slot == 0, order.astype(jnp.int32), codes)
        info = jnp.where(slot == 2, here.astype(jnp.int32), info)
        needed = jnp.max(jnp.where(code < per, 0, (code - per) // 4 + 1), axis=1, keepdims=True)
        info_ref[...] = jnp.where(slot == 3, needed, info)


def schedule(me, session, slots, first, last, before=()):
    count = session.shape[1]
    nodes = count // slots
    vmem = pl.BlockSpec(memory_space=pltpu.VMEM)
    done = pl.pallas_call(
        functools.partial(schedule_kernel, first, last, slots),
        in_specs=[pl.BlockSpec(memory_space=pltpu.SMEM)] + [vmem] * (1 + len(before)),
        out_shape=[
            jax.ShapeDtypeStruct((nodes, 128), jnp.int32),
            jax.ShapeDtypeStruct((8, count), jnp.int32),
            jax.ShapeDtypeStruct((1, 128), jnp.int32),
            jax.ShapeDtypeStruct((nodes, 128), jnp.int32),
        ],
        compiler_params=params(),
        cost_estimate=cost(10**7, 2**20),
        name="schedule",
    )(me.reshape(1), session, *before)
    return done[:2], done[2], done[3]


def item_copies(code, pages, state, pool, target, sem):
    local = state.shape[0]
    rows = state.shape[1]
    per = pages.shape[0] // local
    tokens = pool.shape[1]

    @pl.when((code >= 0) & (code < local))
    def _():
        pltpu.make_async_copy(state.at[code], target.at[pl.ds(0, rows)], sem).start()
        for m in range(per):
            pltpu.make_async_copy(
                pool.at[pages[code * per + m]],
                target.at[pl.ds(rows + m * tokens, tokens)],
                sem,
            ).start()


def session_step(held, x, bc, ct, cd, gate, queries, new, fixed, prefix, results):
    gated, squares, fresh, out = results
    heads, width, depth = fresh.shape
    rows = heads * width
    attend_step(held[rows:], queries[...], new[...], prefix, out)
    mamba_step(
        held[:rows].reshape(heads, width, depth),
        x[...], bc[...], ct[...], cd[...], *[f[...] for f in fixed], gate[...],
        gated, squares, fresh,
    )


def info_order(info, at):
    return info[at, 0]


def info_code(info, s):
    return info[s, 1]


def done_before(info, t):
    done = 0
    for u in range(FROM, t):
        done = jnp.minimum(info[u, 2], done + TOGETHER)
    return done


def span(info, t):
    if t < STEPS[0]:
        return done_before(info, t), done_before(info, t + 1)
    if t == STEPS[0]:
        return done_before(info, t), info[t, 2]
    return info[STEPS[0], 2], 16


class Sessions:
    def __init__(self, info, prefix, pages, fixed, state, pool, inputs, received, late, results, scratch):
        self.info, self.prefix, self.pages, self.fixed = info, prefix, pages, fixed
        self.state, self.pool, self.received, self.late = state, pool, received, late
        self.inputs, self.results = inputs, results
        kinds = len(inputs)
        self.item, self.blocks, self.places = scratch[0], scratch[1 : 1 + kinds], scratch[1 + kinds : -3]
        self.item_sem, self.in_sem, self.out_sem = scratch[-3:]

    @staticmethod
    def part(ref, s, block):
        size = block.shape[0]
        if len(ref.shape) == len(block.shape):
            return ref.at[pl.ds(pl.multiple_of(s * size, size), size)]
        return ref.at[s]

    def fetches(self, at):
        s, k = info_order(self.info, at), at % 2
        return [
            pltpu.make_async_copy(self.part(ref, s, block.at[k]), block.at[k], self.in_sem.at[k, n])
            for n, (ref, block) in enumerate(zip(self.inputs, self.blocks))
        ]

    def stores(self, at):
        s, k = info_order(self.info, at), at % 2
        return [
            pltpu.make_async_copy(place.at[k], self.part(ref, s, place.at[k]), self.out_sem.at[k, n])
            for n, (ref, place) in enumerate(zip(self.results, self.places))
        ]

    def fetch(self, at):
        s = info_order(self.info, at)
        code = info_code(self.info, s)
        target, sem = self.item.at[at % 2], self.item_sem.at[at % 2]
        item_copies(code, self.pages, self.state, self.pool, target, sem)
        for b, source in enumerate(self.received):

            @pl.when(code == self.state.shape[0] + b)
            def _(source=source):
                pltpu.make_async_copy(source, target, sem).start()

        if self.late is not None:

            @pl.when(code == LOST)
            def _():
                pltpu.make_async_copy(self.late.at[s], target, sem).start()

        for copy in self.fetches(at):
            copy.start()

    def begin(self, lo, hi):
        @pl.when(lo < hi)
        def _():
            self.fetch(lo)

    def run(self, lo, hi):
        def settle(at):
            for copy in self.stores(at):
                copy.wait()

        def body(at, carry):
            @pl.when(at + 1 < hi)
            def _():
                self.fetch(at + 1)

            for copy in self.fetches(at):
                copy.wait()
            k = at % 2
            pltpu.make_async_copy(self.item.at[k], self.item.at[k], self.item_sem.at[k]).wait()

            @pl.when(at - 2 >= lo)
            def _():
                settle(at - 2)

            session_step(
                self.item.at[k], *[block.at[k] for block in self.blocks], self.fixed,
                self.prefix[info_order(self.info, at)], [place.at[k] for place in self.places],
            )
            for copy in self.stores(at):
                copy.start()
            return carry

        lax.fori_loop(lo, hi, body, 0)
        for back in (2, 1):

            @pl.when(hi - back >= lo)
            def _(back=back):
                settle(hi - back)


def session_scratch(slots, item, inputs, results):
    def block(a):
        each = (a.shape[0] // slots,) if len(a.shape) == 2 else ()
        return pltpu.VMEM((2,) + each + a.shape[1:], a.dtype)

    return (
        [pltpu.VMEM((2,) + item, BF16)]
        + [block(a) for a in inputs]
        + [block(a) for a in results]
        + [
            pltpu.SemaphoreType.DMA((2,)),
            pltpu.SemaphoreType.DMA((2, len(inputs))),
            pltpu.SemaphoreType.DMA((2, len(results))),
        ]
    )


def gather_kernel(t, kinds, tokens, codes, info, prefix, pages, *refs):
    refs = list(refs)

    def take(count):
        got = refs[:count]
        del refs[:count]
        return got

    fixed = take(4) if kinds else []
    state, pool = take(2)
    take(tokens)
    inputs = take(kinds)
    if kinds:
        take(4)
    received = take(len(refs) - (4 + 3 + (4 + kinds + 8 if kinds else 0)))
    targets = take(4)
    results = take(4) if kinds else []
    held, sem, out_sem = take(3)
    local = state.shape[0]
    wanted = [codes[0, 4 * t + d] for d in range(4)]

    def load(d, carry):
        item_copies(codes[0, 4 * t + d], pages, state, pool, held.at[d], sem.at[d])
        return carry

    lax.fori_loop(0, 4, load, 0)
    for b, source in enumerate(received):
        hits = [(code == local + b).astype(jnp.int32) for code in wanted]

        @pl.when(hits[0] + hits[1] + hits[2] + hits[3] > 0)
        def _(source=source, d=hits[1] + 2 * hits[2] + 3 * hits[3]):
            pltpu.make_async_copy(source, held.at[d], sem.at[d]).start()

    if kinds:
        work = Sessions(
            info, prefix, pages, fixed, state, pool, inputs, received, None, results, refs
        )
        lo, hi = span(info, t)
        work.begin(lo, hi)

    def store(d):
        return pltpu.make_async_copy(held.at[d], targets[d], out_sem.at[d])

    for d in range(4):

        @pl.when(wanted[d] >= 0)
        def _(d=d):
            pltpu.make_async_copy(held.at[d], held.at[d], sem.at[d]).wait()
            store(d).start()

    if kinds:
        work.run(lo, hi)
    for d in range(4):

        @pl.when(wanted[d] >= 0)
        def _(d=d):
            store(d).wait()


def gather(
    t, codes, info, prefix, pages, state, pool, tokens, received, fixed=(), inputs=(), results=()
):
    slots = state.shape[0]
    rows = state.shape[1] + pages.shape[0] // slots * pool.shape[1]
    smem = pl.BlockSpec(memory_space=pltpu.SMEM)
    anywhere = pl.BlockSpec(memory_space=pl.ANY)
    hbm = pl.BlockSpec(memory_space=pltpu.HBM)
    item = (rows, state.shape[2])
    out = jax.ShapeDtypeStruct(item, state.dtype)
    scratch = [
        pltpu.VMEM((4,) + item, state.dtype),
        pltpu.SemaphoreType.DMA((4,)),
        pltpu.SemaphoreType.DMA((4,)),
    ]
    kinds = len(inputs)
    first = 4 + len(fixed) + 2 + len(tokens) + kinds
    if kinds:
        scratch += session_scratch(slots, item, inputs, results)
    done = pl.pallas_call(
        functools.partial(gather_kernel, t, kinds, len(tokens)),
        in_specs=[smem] * 4
        + [pl.BlockSpec(memory_space=pltpu.VMEM)] * len(fixed)
        + [anywhere] * (2 + len(tokens) + kinds)
        + [hbm] * len(results)
        + [anywhere] * len(received),
        out_specs=[hbm] * (4 + len(results)),
        out_shape=[out] * 4 + [jax.ShapeDtypeStruct(a.shape, a.dtype) for a in results],
        input_output_aliases={first + n: 4 + n for n in range(len(results))},
        scratch_shapes=scratch,
        compiler_params=params(),
        cost_estimate=cost(10**8, 16 * rows * state.shape[2]),
        name="gather_step",
    )(codes, info, prefix, pages, *fixed, state, pool, *tokens, *inputs, *results, *received)
    return done[:4], done[4:]


def sessions_kernel(t, kinds, last, info, prefix, pages, *refs):
    fixed, (state, pool), refs = refs[:4], refs[4:6], refs[6:]
    inputs, refs = refs[:kinds], refs[kinds + 4 :]
    scratch, refs = refs[-(4 + kinds + 4) :], refs[: -(4 + kinds + 4)]
    results, received = refs[-4:], refs[:-4]
    received, late = (received[:-1], received[-1]) if last else (received, None)
    work = Sessions(
        info, prefix, pages, fixed, state, pool, inputs, received, late, results, scratch
    )
    lo, hi = span(info, t)
    work.begin(lo, hi)
    work.run(lo, hi)


def sessions(t, info, prefix, pages, fixed, state, pool, inputs, results, received, late=()):
    slots = state.shape[0]
    smem = pl.BlockSpec(memory_space=pltpu.SMEM)
    anywhere = pl.BlockSpec(memory_space=pl.ANY)
    hbm = pl.BlockSpec(memory_space=pltpu.HBM)
    kinds = len(inputs)
    first = 3 + len(fixed) + 2 + kinds
    return pl.pallas_call(
        functools.partial(sessions_kernel, t, kinds, len(late) > 0),
        in_specs=[smem] * 3
        + [pl.BlockSpec(memory_space=pltpu.VMEM)] * len(fixed)
        + [anywhere] * (2 + kinds)
        + [hbm] * len(results)
        + [anywhere] * (len(received) + len(late)),
        out_specs=[hbm] * len(results),
        out_shape=[jax.ShapeDtypeStruct(a.shape, a.dtype) for a in results],
        input_output_aliases={first + n: n for n in range(len(results))},
        scratch_shapes=session_scratch(slots, received[0].shape, inputs, results),
        compiler_params=params(),
        cost_estimate=cost(2 * 10**9, 32 * 2**20),
        name="sessions",
    )(info, prefix, pages, *fixed, state, pool, *inputs, *results, *received, *late)


def blank_kernel(*refs):
    pass


def blank(shapes):
    hbm = pl.BlockSpec(memory_space=pltpu.HBM)
    return pl.pallas_call(
        blank_kernel,
        out_specs=[hbm] * len(shapes),
        out_shape=shapes,
        compiler_params=params(),
        name="blank",
    )()


def shift(block, direction):
    route = []
    for n in range(lax.axis_size("sess")):
        y, x = n // SIDE, n % SIDE
        if direction < 2:
            x = (x + 1 - 2 * direction) % SIDE
        else:
            y = (y + 1 - 2 * (direction - 2)) % SIDE
        route.append((n, y * SIDE + x))
    return lax.ppermute(block, "sess", route)


def shards(
    mamba_x,
    gate_z,
    proj_bc,
    step_raw,
    step_bias,
    decay_log,
    skip_gain,
    norm_gain,
    state_cache,
    cache_slot,
    prefix_pages,
    page_table,
    queries,
    appended_memory_pair,
    key_value_pages,
):
    slots, heads = state_cache.shape[:2]
    count = cache_slot.shape[0]
    total, wide = mamba_x.shape
    tokens = total // slots
    me = lax.axis_index("sess")
    nodes = count // slots
    names = jnp.arange(count, dtype=jnp.int32)
    holds = (cache_slot[:, None] == names[None, :]).astype(jnp.int32)
    session = jnp.sum(holds * names[:, None], axis=0, keepdims=True)

    plans, routed = [], ()
    for start, end in zip((0,) + PARTS, PARTS):
        routed, plan, info = schedule(me, session, slots, start, end, routed)
        plans += [plan] * (end - start)
    items = routed[1]
    final = items[5]
    needed = info[0, 3]
    local = jnp.arange(slots, dtype=jnp.int32)
    at_home = (cache_slot[:, None] == (me * slots + local)[None, :]).astype(jnp.int32)
    pages = jnp.sum(at_home[:, :, None] * page_table[:, None, :], axis=0).reshape(-1)

    pool = key_value_pages.reshape(key_value_pages.shape[:2] + (2 * HEAD_WIDTH,))
    state = state_cache.reshape(slots, heads * P_SIZE, NS)
    item = (heads * P_SIZE + page_table.shape[1] * PAGE_TOKENS, NS)

    group = lax.axis_index("mp") * heads // (HM // G)
    both = lax.dynamic_index_in_dim(proj_bc, group, axis=2, keepdims=False)
    ct, cd = prepare(step_raw, step_bias, decay_log, slots)
    quads = jnp.repeat(jnp.repeat(jnp.eye(4, dtype=BF16), tokens, axis=0), P_SIZE, axis=1)
    fixed = (skip_gain[None, :], spread_matrix(heads, tokens), spread_matrix(heads, P_SIZE), quads)
    new = appended_memory_pair.reshape(total, 2 * HEAD_WIDTH)
    inputs = (mamba_x, both.reshape(total, 2 * NS), ct, cd, gate_z, queries, new)
    ahead = {2: (ct, new), 4: (inputs[1],), 5: (plans[6],)}
    results = blank(
        [
            jax.ShapeDtypeStruct((total, wide), F32),
            jax.ShapeDtypeStruct((slots, tokens, 128), F32),
            jax.ShapeDtypeStruct(state_cache.shape, BF16),
            jax.ShapeDtypeStruct((total, wide), BF16),
        ]
    )

    def step(t, marks, received, inputs=(), results=()):
        ready = received[: 4 * max(0, t - DELAY)]
        sent, results = gather(
            t, plans[t], info if inputs else plans[t], prefix_pages, pages, state, pool, marks,
            ready, fixed if inputs else (), inputs, results,
        )
        got = []
        for d, block in enumerate(sent):
            got.append(shift(block, d))
        return sent, received + got, results

    sent, received = [pool], []
    for t in range(STEPS[0]):
        marks = [sent[0]] + list(ahead.get(t, ())) + (received[-4:-3] if t == STEPS[0] - 1 else [])
        if t < FROM:
            sent, received, _ = step(t, marks, received)
        else:
            sent, received, results = step(t, marks, received, inputs, results)

    def deliver(received, held):
        def body(carry):
            left, held = carry
            c = jnp.argmax(left)
            code = items[2][c]
            plan = jnp.stack([code, -1, -1, -1])[None]
            block = gather(
                0, plan, plan, prefix_pages, pages, state, pool, (), received
            )[0][0]
            to = session[0][c]
            place = to % slots
            old = lax.dynamic_index_in_dim(held, place, 0, keepdims=False)
            ring = [(n, (n + 1) % nodes) for n in range(nodes)]

            def turn(r, carry):
                block, kept = carry
                block = lax.ppermute(block, "sess", ring)
                mine = (to // slots == me) & ((items[4][c] + r) % nodes == me)
                return block, jnp.where(mine, block, kept)

            block = lax.fori_loop(1, nodes, turn, (block, old))[1]
            held = lax.dynamic_update_index_in_dim(held, block, place, 0)
            return left.at[c].set(0), held

        left = (final == LOST).astype(jnp.int32)
        return lax.while_loop(lambda carry: jnp.max(carry[0]) > 0, body, (left, held))[1]

    def shapes(t):
        kinds = [jax.ShapeDtypeStruct(item, BF16)] * (4 * (STEPS[1] - t))
        return kinds + [jax.ShapeDtypeStruct((slots,) + item, BF16)]

    def late_steps(t, received):
        if t == STEPS[1]:
            return [deliver(received, blank(shapes(t))[0])]

        def more(_):
            after = step(t, (), received)[1]
            return after[4 * t :] + late_steps(t + 1, after)

        return list(lax.cond(needed > t, more, lambda _: list(blank(shapes(t))), 0))

    results = sessions(
        STEPS[0], info, prefix_pages, pages, fixed, state, pool, inputs, results, received[:-4]
    )
    rest = late_steps(STEPS[0], received)
    received, late = received + rest[:-1], rest[-1]

    gated, squares, fresh, out = sessions(
        STEPS[1], info, prefix_pages, pages, fixed, state, pool, inputs, results, received, [late]
    )
    squares = squares[:, :, 0].reshape(total)
    squares = squares + swapped(squares, "mp", 0)
    scale = lax.rsqrt(squares / (HM // G * P_SIZE) + EPS)
    mixed = (gated * scale[:, None] * norm_gain[None, :]).astype(BF16)
    return mixed, fresh, out


def solution(mesh):
    return jax.shard_map(
        shards,
        mesh=mesh,
        in_specs=(
            P("sess", "mp"),
            P("sess", "mp"),
            P("sess", None, None, None),
            P("mp", "sess"),
            P("mp"),
            P("mp"),
            P("mp"),
            P("mp"),
            P("sess", "mp", None, None),
            P(),
            P("sess"),
            P(),
            P("sess", "mp"),
            P("sess", None, "mp", None),
            P("sess", None, None, "mp", None),
        ),
        out_specs=(P("sess", "mp"), P("sess", "mp", None, None), P("sess", "mp")),
        check_vma=False,
    )
```
